512 devices in a mesh: dp: 64 (over z, x, core), tensor: 8 (over y).
Axes of the slice: x: 4, y: 8, z: 8, core: 2. Of those that a mesh axis runs over, the one named last changes fastest.
Arguments:
- gradients: bfloat16 [16384, 14336], P('dp', 'tensor'), may hold values from -40 to 40
- errors: bfloat16 [16384, 14336], P('dp', 'tensor'), may hold values from -3 to 3
- warm_factor: bfloat16 [64, 14336], P(None, 'tensor'), may hold values from -5 to 5
Outputs:
- new_errors: bfloat16 [16384, 14336], P('dp', 'tensor')
- left_factor: float32 [64, 4096], P(None, 'dp')
- right_factor: bfloat16 [64, 14336], P(None, 'tensor')
The draws below stay inside these ranges and needn't reach their ends.
All inputs are finite; a program needn't handle non-finite values.
Results may differ from the reference program's by a relative error of at most 0.0071.
Values may be sent and summed in bfloat16 or wider, within the bound.
A program may use at most 64 MiB of HBM per device.

```python
import math
import jax
import jax.numpy as jnp
from jax import lax

FF = 14336
ROWS = 4096
RANK = 64
ITERS = 2
STACK = 16384


def draw_gradients(key, part):
    key = jax.random.fold_in(key, 11)
    first, second, third, fourth = jax.random.split(key, 4)
    replicas = STACK // ROWS
    row_scale = jnp.exp(jax.random.uniform(first, (1, ROWS, 1), jnp.float32, math.log(0.5), math.log(5.0)))
    col_scale = jnp.exp(jax.random.uniform(second, (1, 1, FF), jnp.float32, math.log(0.7), math.log(1.4)))
    common = jnp.clip(jax.random.normal(third, (1, ROWS, FF), jnp.float32), -4.0, 4.0)
    replica_noise = jnp.clip(jax.random.normal(fourth, (replicas, ROWS, FF), jnp.float32), -4.0, 4.0)
    shared_weight = 0.25
    owner = jnp.arange(replicas, dtype=jnp.int32).reshape(replicas, 1, 1)
    row_owner = (jnp.arange(ROWS, dtype=jnp.int32) // (ROWS // replicas)).reshape(1, ROWS, 1)
    col_owner = (jnp.arange(FF, dtype=jnp.int32) // (FF // replicas)).reshape(1, 1, FF)
    boost = 1.0 + 3.0 * jnp.logical_or(row_owner == owner, col_owner == owner).astype(jnp.float32)
    stacked = (shared_weight * common + boost * replica_noise) * row_scale * col_scale
    stacked = jnp.clip(stacked, -40.0, 40.0)
    return stacked.reshape(STACK, FF).astype(jnp.bfloat16)


def shard_levels(stream_key, dims, pieces, low, largest):
    factor_of = 1.0
    for axis_at, blocks in pieces:
        draws = jax.random.uniform(jax.random.fold_in(jax.random.fold_in(stream_key, 6), axis_at), (blocks,), jnp.float32, low / len(pieces), largest / len(pieces))
        factor_of = factor_of * jnp.repeat(jnp.exp(draws), dims[axis_at] // blocks).reshape((-1,) + (1,) * (len(dims) - 1 - axis_at))
    return factor_of


def scatter_about(own_key, dims, width, reach, pieces=(), kind=jnp.bfloat16):
    drawn = jax.random.normal(own_key, dims, jnp.float32) * width
    if len(pieces) > 0:
        drawn = shard_levels(own_key, dims, pieces, -0.22, 0.18) * drawn
    return jnp.clip(drawn, min=-reach, max=reach).astype(kind)


def setup_inputs(seed: int = 0) -> dict:
    seeds = jax.random.split(jax.random.key(seed), 4)
    gradients = draw_gradients(jax.random.fold_in(seeds[3], 71), 0)
    errors = scatter_about(seeds[1], (STACK, FF), 0.5, 3.0, ((0, 64), (1, 8)))
    warm_factor = scatter_about(seeds[2], (RANK, FF), 1.0, 5.0, ((1, 8),))
    return dict(gradients=gradients, errors=errors, warm_factor=warm_factor)


def orthonormal(p_summed):
    gram_matrix = lax.dot_general(p_summed.astype(jnp.float32), p_summed.astype(jnp.float32), (((1,), (1,)), ((), ())), precision=lax.Precision.HIGHEST, preferred_element_type=jnp.float32)
    lower_factor = jnp.linalg.cholesky(gram_matrix)
    return lax.linalg.triangular_solve(lower_factor, p_summed, left_side=True, lower=True)

def reference(gradients, errors, warm_factor):
    replicas = STACK // ROWS
    grad_blocks = gradients.reshape(replicas, ROWS, FF)
    error_blocks = errors.reshape(replicas, ROWS, FF)
    corrected = (grad_blocks.astype(jnp.float32) + error_blocks.astype(jnp.float32)).astype(jnp.bfloat16)
    q_rounded = warm_factor
    p_rounded = None
    left_factor = None
    for iteration in range(ITERS):

        def add_left(running, corrected_block):
            term = lax.dot_general(q_rounded.astype(jnp.float32), corrected_block.astype(jnp.float32), (((1,), (1,)), ((), ())), preferred_element_type=jnp.float32)
            return (running + term, None)
        p_summed, _ = lax.scan(add_left, jnp.zeros((RANK, ROWS), jnp.float32), corrected)
        left_factor = orthonormal(p_summed)
        p_rounded = left_factor.astype(jnp.bfloat16)

        def add_right(running, corrected_block):
            return (running + jnp.dot(p_rounded.astype(jnp.float32), corrected_block.astype(jnp.float32), preferred_element_type=jnp.float32), None)
        q_summed, _ = lax.scan(add_right, jnp.zeros((RANK, FF), jnp.float32), corrected)
        q_rounded = (q_summed / replicas).astype(jnp.bfloat16)
    rebuilt = lax.dot_general(p_rounded.astype(jnp.float32), q_rounded.astype(jnp.float32), (((0,), (0,)), ((), ())), preferred_element_type=jnp.float32)

    def renew(pair):
        grad_block, error_block = pair
        return (grad_block.astype(jnp.float32) + error_block.astype(jnp.float32) - rebuilt).astype(jnp.bfloat16)
    new_errors = lax.map(renew, (grad_blocks, error_blocks)).reshape(STACK, FF)
    return (new_errors, left_factor, q_rounded)
```

```python
import functools

import jax
import jax.numpy as jnp
from jax import lax
from jax.experimental import pallas as pl
from jax.experimental.pallas import tpu as pltpu
from jax.sharding import PartitionSpec as P

ITERS = 2
MESH = pl.DeviceIdType.MESH
HIGH = lax.Precision.HIGHEST
F32 = jnp.float32
BF16 = jnp.bfloat16
RANK = 64


def lanes(shape):
    return lax.broadcasted_iota(jnp.int32, shape, 1)


def spread(x):
    low = lanes(x.shape) < RANK
    turned = pltpu.roll(x, RANK, 1)
    zero = jnp.zeros_like(x)
    first = jnp.concatenate([jnp.where(low, x, zero), jnp.where(low, turned, zero)], axis=0)
    second = jnp.concatenate([jnp.where(low, zero, turned), jnp.where(low, zero, x)], axis=0)
    return first, second


def split3(x):
    hi = x.astype(BF16)
    rest = x - hi.astype(F32)
    mid = rest.astype(BF16)
    return hi, mid, (rest - mid.astype(F32)).astype(BF16)


def nt(a, b):
    return lax.dot_general(a, b, (((1,), (1,)), ((), ())), precision=HIGH, preferred_element_type=F32)


def eliminate(rows, first, last, out_ref):
    block = 8
    for k0 in range(first, last, block):
        n = rows.shape[0]
        cols = [jnp.broadcast_to(rows[:, k0 + j : k0 + j + 1], (n, 128)) for j in range(block)]
        for i in range(block):
            pivot = cols[i][i : i + 1, :]
            row = rows[i : i + 1, :]
            out_ref[k0 + i : k0 + i + 1, :] = row * lax.rsqrt(pivot)
            if k0 + i == RANK - 1:
                break
            factor = cols[i] * (1.0 / pivot)
            rows = rows - factor * row
            for j in range(i + 1, block):
                cols[j] = cols[j] - factor * cols[j][i : i + 1, :]
        rows = rows[block:, :] if n > block else rows
    return rows


def kernel(
    geo, g_hbm, e_hbm, w_ref, ne_hbm, left_ref, right_ref,
    gv, ev, cv, ctv, nev,
    p_send, p_rs, p_z, p_ag, g_send, g_x, g_ag, chol,
    q_send, q_core, q_zs, q_z, q_xs, q_x, q_ag, l_send, l_recv,
    load_sem, store_sem,
    prs_s, prs_r, pz_s, pz_r, pag_s, pag_r, gx_s, gx_r, gag_s, gag_r,
    qc_s, qc_r, qz_s, qz_r, qx_s, qx_r, ax_s, ax_r, az_s, az_r, ac_s, ac_r, l_sem,
):
    nz, nx, nc, ny, owners = geo
    nb = nx * nc
    dp, y = lax.axis_index("dp"), lax.axis_index("tensor")
    c = lax.rem(dp, nc)
    b = lax.rem(dp, nb)
    x = lax.div(b, nc)
    z = lax.div(dp, nb)
    rows, cols = gv.shape
    half_rows, half = rows // 2, cols // 2

    def at(zz, bb, yy):
        return (zz * nb + bb, yy)

    def y_dev(j):
        return at(z, b, j)

    def z_dev(j):
        return at(j, b, y)

    def b_dev(j):
        return at(z, j, y)

    def x_dev(j):
        return at(z, j * nc + c, y)

    partner = at(z, x * nc + (1 - c), y)
    l_dst = nz * b + z
    l_src = lax.rem(dp, nz) * nb + lax.div(dp, nz)
    moved = l_dst != dp

    loads = [
        pltpu.make_async_copy(g_hbm, gv, load_sem.at[0]),
        pltpu.make_async_copy(e_hbm, ev, load_sem.at[1]),
    ]
    for load in loads:
        load.start()

    barrier = pltpu.get_barrier_semaphore()
    for n, me, dev in ((ny, y, y_dev), (nz, z, z_dev), (nb, b, b_dev)):
        for k in range(1, n):
            pl.semaphore_signal(barrier, inc=1, device_id=dev(lax.rem(me + k, n)), device_id_type=MESH)

    @pl.when(moved)
    def _():
        pl.semaphore_signal(barrier, inc=1, device_id=(l_dst, y), device_id_type=MESH)
        pl.semaphore_signal(barrier, inc=1, device_id=(l_src, y), device_id_type=MESH)

    def remote(src, dst, send, recv, dev):
        return pltpu.make_async_remote_copy(
            src_ref=src, dst_ref=dst, send_sem=send, recv_sem=recv, device_id=dev, device_id_type=MESH
        )

    def far_first(n):
        return sorted(range(1, n), key=lambda k: -min(k, n - k))

    def push(n, me, dev, src, dst, send, recv):
        for k in far_first(n):
            j = lax.rem(me + k, n)
            remote(src(j), dst, send.at[k], recv.at[me], dev(j)).start()

    def pull(n, me, dev, dst, send, recv):
        for k in far_first(n)[::-1]:
            j = lax.rem(me + k, n)
            remote(dst(j), dst(j), send.at[k], recv.at[j], dev(j)).wait_recv()

    def drain(n, me, dev, src, dst, send, recv):
        for k in range(1, n):
            j = lax.rem(me + k, n)
            remote(src(j), dst, send.at[k], recv.at[me], dev(j)).wait_send()

    pending = []

    def swap(n, me, dev, src, dst, send, recv):
        push(n, me, dev, src, dst(me), send, recv)
        pending.append(lambda: drain(n, me, dev, src, dst(me), send, recv))
        return lambda: pull(n, me, dev, dst, send, recv)

    q_packed = jnp.concatenate([w_ref[:, :half], w_ref[:, half:]], axis=0).T
    for load in loads:
        load.wait()
    cv[...] = (gv[...].astype(F32) + ev[...].astype(F32)).astype(BF16)

    for it in range(ITERS):
        last = it == ITERS - 1
        one = jnp.dot(cv[:, :half], q_packed, preferred_element_type=F32)
        two = jnp.dot(cv[:, half:], q_packed, preferred_element_type=F32)
        low = lanes((half_rows, 128)) < RANK
        packed = jnp.where(
            low,
            one[:half_rows] + pltpu.roll(two[:half_rows], RANK, 1),
            pltpu.roll(one[half_rows:], RANK, 1) + two[half_rows:],
        )
        p_send[it] = packed.reshape(ny, half_rows // ny, 128)
        if it == 0:
            pl.semaphore_wait(barrier, ny - 1 + nz - 1 + nb - 1 + jnp.where(moved, 2, 0))

        wait = swap(
            ny, y, y_dev, lambda j: p_send.at[it, j], lambda j: p_rs.at[it, j], prs_s.at[it], prs_r.at[it]
        )
        p_rs[it, y] = p_send[it, y]
        if it == 0:
            ctv[...] = cv[...].T.reshape(ctv.shape)
        wait()
        p_z[it, z] = functools.reduce(jnp.add, [p_rs[it, j] for j in range(ny)])
        wait = swap(nz, z, z_dev, lambda j: p_z.at[it, z], lambda j: p_z.at[it, j], pz_s.at[it], pz_r.at[it])
        wait()
        p_ag[it, y] = functools.reduce(jnp.add, [p_z[it, j] for j in range(nz)])
        wait = swap(ny, y, y_dev, lambda j: p_ag.at[it, y], lambda j: p_ag.at[it, j], pag_s.at[it], pag_r.at[it])
        wait()
        p_whole = p_ag[it].reshape(half_rows, 128)

        gram2 = lax.dot_general(
            p_whole, p_whole, (((0,), (0,)), ((), ())), precision=HIGH, preferred_element_type=F32
        )
        gram = gram2[:RANK] + pltpu.roll(gram2[RANK:], RANK, 1)
        g_send[it] = gram.reshape(g_send.shape[1:])
        g_x[it, b] = g_send[it, y]
        wait_gram = swap(nb, b, b_dev, lambda j: g_x.at[it, b], lambda j: g_x.at[it, j], gx_s.at[it], gx_r.at[it])

        first, second = spread(p_whole)
        terms = list(zip(split3(first), split3(second)))

        def right_term(core):
            total = None
            for one_p, two_p in terms:
                term = jnp.dot(ctv[0, core], one_p, preferred_element_type=F32)
                term += jnp.dot(ctv[1, core], two_p, preferred_element_type=F32)
                total = term if total is None else total + term
            return total

        q_send[it, 1 - c] = right_term(1 - c)
        half_copy = remote(q_send.at[it, 1 - c], q_core.at[it], qc_s.at[it], qc_r.at[it], partner)
        half_copy.start()
        pending.append(half_copy.wait_send)

        wait_gram()
        g_ag[it, y] = functools.reduce(jnp.add, [g_x[it, j] for j in range(nb)])
        wait_gram = swap(ny, y, y_dev, lambda j: g_ag.at[it, y], lambda j: g_ag.at[it, j], gag_s.at[it], gag_r.at[it])

        own_half = right_term(c)
        half_copy.wait_recv()
        q_zs[it] = (own_half + q_core[it]).reshape(q_zs.shape[1:])
        wait_z = swap(nz, z, z_dev, lambda j: q_zs.at[it, j], lambda j: q_z.at[it, j], qz_s.at[it], qz_r.at[it])

        wait_gram()
        gram = g_ag[it].reshape(RANK, 128)
        lane = lanes((RANK, 128))
        unit = (lane - RANK == lax.broadcasted_iota(jnp.int32, (RANK, 128), 0)).astype(F32)
        work = jnp.where(lane < RANK, gram, unit)
        work = eliminate(work, 0, RANK // 2, chol)

        wait_z()
        total = q_zs[it, z]
        for k in range(1, nz):
            total = total + q_z[it, lax.rem(z + k, nz)]
        q_xs[it] = total.reshape(q_xs.shape[1:])
        for k in far_first(nx):
            j = lax.rem(x + k, nx)

            @pl.when(j < owners)
            def _(k=k, j=j):
                remote(q_xs.at[it, j], q_x.at[it, x], qx_s.at[it, k], qx_r.at[it, x], x_dev(j)).start()

        eliminate(work, RANK // 2, RANK, chol)
        inverse = chol[...]
        turned = pltpu.roll(inverse, RANK, 1)
        solve = jnp.concatenate([jnp.where(lane < RANK, turned, 0.0), jnp.where(lane < RANK, 0.0, inverse)], axis=0)

        @pl.when(x < owners)
        def _():
            total = q_xs[it, x]
            for k in range(1, nx):
                j = lax.rem(x + k, nx)
                remote(q_x.at[it, j], q_x.at[it, j], qx_s.at[it, k], qx_r.at[it, j], x_dev(j)).wait_recv()
            for k in range(1, nx):
                total = total + q_x[it, lax.rem(x + k, nx)]
            mine = q_ag.at[it, c, z, x]
            mine[...] = (nt(total, solve) / nz).astype(BF16)
            for k in far_first(nx):
                remote(mine, mine, ax_s.at[it, k], ax_r.at[it, x], x_dev(lax.rem(x + k, nx))).start()

        if last:
            left = nt(p_whole, solve)
            turned_left = left.T
            per_half = nz // 2
            wide = rows // nz
            for zz in range(nz):
                h, o = zz // per_half, zz % per_half * wide
                l_send[zz] = turned_left[h * RANK : (h + 1) * RANK, o : o + wide]
            l_copy = remote(l_send.at[z], l_recv, l_sem.at[0], l_sem.at[1], (l_dst, y))

            @pl.when(moved)
            def _():
                l_copy.start()

            @pl.when(jnp.logical_not(moved))
            def _():
                l_recv[...] = l_send[z]

            p_first, p_second = spread(left)
            p_first, p_second = p_first.astype(BF16), p_second.astype(BF16)

        for k in range(1, nx):
            j = lax.rem(x + k, nx)

            @pl.when(j < owners)
            def _(k=k, j=j):
                slot = q_ag.at[it, c, z, j]
                remote(slot, slot, ax_s.at[it, k], ax_r.at[it, j], x_dev(j)).wait_recv()

        swap(nz, z, z_dev, lambda j: q_ag.at[it, c, z], lambda j: q_ag.at[it, c, j], az_s.at[it], az_r.at[it])()
        all_copy = remote(q_ag.at[it, c], q_ag.at[it, c], ac_s.at[it], ac_r.at[it], partner)
        all_copy.start()
        pending.append(all_copy.wait_send)
        other = q_ag.at[it, 1 - c]
        remote(other, other, ac_s.at[it], ac_r.at[it], partner).wait_recv()
        q_packed = q_ag[it].reshape(half, 128)

    q_turned = q_packed.T
    right_ref[:, :half] = q_turned[:RANK]
    right_ref[:, half:] = q_turned[RANK:]
    stores = []
    for at_half, left_half in ((0, p_first), (half, p_second)):
        span = slice(at_half, at_half + half)
        rebuilt = jnp.dot(left_half, q_turned, preferred_element_type=F32)
        nev[:, span] = (gv[:, span].astype(F32) + ev[:, span].astype(F32) - rebuilt).astype(BF16)
        stores.append(pltpu.make_async_copy(nev.at[:, span], ne_hbm.at[:, span], store_sem.at[len(stores)]))
        stores[-1].start()

    @pl.when(moved)
    def _():
        l_copy.wait()

    left_ref[...] = l_recv[...]
    for it in range(ITERS):
        for k in range(1, nx):
            j = lax.rem(x + k, nx)

            @pl.when(j < owners)
            def _(it=it, k=k, j=j):
                remote(q_xs.at[it, j], q_x.at[it, x], qx_s.at[it, k], qx_r.at[it, x], x_dev(j)).wait_send()

            @pl.when(x < owners)
            def _(it=it, k=k, j=j):
                mine = q_ag.at[it, c, z, x]
                remote(mine, mine, ax_s.at[it, k], ax_r.at[it, x], x_dev(j)).wait_send()

    for done in pending:
        done()
    for store in stores:
        store.wait()


def step(geo, gradients, errors, warm_factor):
    nz, nx, nc, ny, owners = geo
    nb = nx * nc
    rows, cols = gradients.shape
    half = cols // 2
    part = rows // 2 // ny
    core_rows = half // nc
    z_rows = core_rows // nz
    x_rows = z_rows // owners
    dma = pltpu.SemaphoreType.DMA
    vmem = pltpu.VMEM
    any_spec = pl.BlockSpec(memory_space=pl.ANY)
    vmem_spec = pl.BlockSpec(memory_space=pltpu.VMEM)
    return pl.pallas_call(
        functools.partial(kernel, geo),
        out_shape=(
            jax.ShapeDtypeStruct((rows, cols), BF16),
            jax.ShapeDtypeStruct((RANK, rows // nz), F32),
            jax.ShapeDtypeStruct((RANK, cols), BF16),
        ),
        in_specs=[any_spec, any_spec, vmem_spec],
        out_specs=(any_spec, vmem_spec, vmem_spec),
        scratch_shapes=[
            vmem((rows, cols), BF16), vmem((rows, cols), BF16), vmem((rows, cols), BF16),
            vmem((2, nc, core_rows, rows), BF16), vmem((rows, cols), BF16),
            vmem((ITERS, ny, part, 128), F32), vmem((ITERS, ny, part, 128), F32),
            vmem((ITERS, nz, part, 128), F32), vmem((ITERS, ny, part, 128), F32),
            vmem((ITERS, ny, RANK // ny, 128), F32), vmem((ITERS, nb, RANK // ny, 128), F32),
            vmem((ITERS, ny, RANK // ny, 128), F32), vmem((RANK, 128), F32),
            vmem((ITERS, nc, core_rows, 128), F32), vmem((ITERS, core_rows, 128), F32),
            vmem((ITERS, nz, z_rows, 128), F32), vmem((ITERS, nz, z_rows, 128), F32),
            vmem((ITERS, owners, x_rows, 128), F32), vmem((ITERS, nx, x_rows, 128), F32),
            vmem((ITERS, nc, nz, owners, x_rows, 128), BF16),
            vmem((nz, RANK, rows // nz), F32), vmem((RANK, rows // nz), F32),
            dma((2,)), dma((2,)),
            dma((ITERS, ny)), dma((ITERS, ny)), dma((ITERS, nz)), dma((ITERS, nz)), dma((ITERS, ny)), dma((ITERS, ny)),
            dma((ITERS, nb)), dma((ITERS, nb)), dma((ITERS, ny)), dma((ITERS, ny)),
            dma((ITERS,)), dma((ITERS,)), dma((ITERS, nz)), dma((ITERS, nz)), dma((ITERS, nx)), dma((ITERS, nx)),
            dma((ITERS, nx)), dma((ITERS, nx)), dma((ITERS, nz)), dma((ITERS, nz)), dma((ITERS,)), dma((ITERS,)),
            dma((2,)),
        ],
        compiler_params=pltpu.CompilerParams(
            collective_id=0, has_side_effects=True, vmem_limit_bytes=40 * 1024 * 1024
        ),
        name="power_step",
    )(gradients, errors, warm_factor)


def build(mesh, geo):
    in_specs = (P("dp", "tensor"), P("dp", "tensor"), P(None, "tensor"))
    out_specs = (P("dp", "tensor"), P(None, "dp"), P(None, "tensor"))
    return jax.shard_map(
        functools.partial(step, geo), mesh=mesh, in_specs=in_specs, out_specs=out_specs, check_vma=False
    )


def solution(mesh):
    return build(mesh, (4, 8, 2, 8, 7))
```

```python
import functools

import jax
import jax.numpy as jnp
from jax import lax
from jax.experimental import pallas as pl
from jax.experimental.pallas import tpu as pltpu
from jax.sharding import PartitionSpec as P

ITERS = 2
MESH = pl.DeviceIdType.MESH
HIGH = lax.Precision.HIGHEST
F32 = jnp.float32
BF16 = jnp.bfloat16
RANK = 64
TILE = 16


def lanes(shape):
    return lax.broadcasted_iota(jnp.int32, shape, 1)


def spread(x):
    low = lanes(x.shape) < RANK
    turned = pltpu.roll(x, RANK, 1)
    zero = jnp.zeros_like(x)
    first = jnp.concatenate([jnp.where(low, x, zero), jnp.where(low, turned, zero)], axis=0)
    second = jnp.concatenate([jnp.where(low, zero, turned), jnp.where(low, zero, x)], axis=0)
    return first, second


def split3(x):
    hi = x.astype(BF16)
    rest = x - hi.astype(F32)
    mid = rest.astype(BF16)
    return hi, mid, (rest - mid.astype(F32)).astype(BF16)


def nt(a, b):
    return lax.dot_general(a, b, (((1,), (1,)), ((), ())), precision=HIGH, preferred_element_type=F32)


def eliminate(rows, out_ref):
    block = 8
    for k0 in range(0, RANK, block):
        n = rows.shape[0]
        cols = [jnp.broadcast_to(rows[:, k0 + j : k0 + j + 1], (n, 128)) for j in range(block)]
        for i in range(block):
            pivot = cols[i][i : i + 1, :]
            row = rows[i : i + 1, :]
            out_ref[k0 + i : k0 + i + 1, :] = row * lax.rsqrt(pivot)
            if k0 + i == RANK - 1:
                break
            factor = cols[i] * (1.0 / pivot)
            rows = rows - factor * row
            for j in range(i + 1, block):
                cols[j] = cols[j] - factor * cols[j][i : i + 1, :]
        rows = rows[block:, :] if n > block else rows


def kernel(
    geo, g_hbm, e_hbm, w_hbm, ne_hbm, left_ref, right_ref,
    gv, ev, wv, cv, ctv, nev,
    p_send, p_rs, p_z, p_ag, g_send, g_x, g_ag, chol,
    q_send, q_core, q_sum, q_x, q_ag, size_ref, l_send, l_recv,
    load_sem, store_sem, send_sem, recv_sem,
):
    nrep, nzl, nx, nc, ny = geo
    nb = nzl * nx * nc
    nz = nrep * nzl
    chips = nz * nx
    owners = q_ag.shape[2]
    dp, y = lax.axis_index("dp"), lax.axis_index("tensor")
    c = lax.rem(dp, nc)
    b = lax.rem(dp, nb)
    rep = lax.div(dp, nb)
    chip = lax.div(dp, nc)
    x = lax.rem(chip, nx)
    z = lax.div(chip, nx)
    rows, cols = gv.shape
    half_rows, half = rows // 2, cols // 2
    partner = (dp + 1 - 2 * c, y)
    l_dst = nrep * b + rep
    l_src = lax.rem(dp, nrep) * nb + lax.div(dp, nrep)
    moved = l_dst != dp

    loads = [
        pltpu.make_async_copy(src, dst, load_sem.at[i])
        for i, (src, dst) in enumerate(((w_hbm, wv), (g_hbm, gv), (e_hbm, ev)))
    ]
    for load in loads:
        load.start()

    def y_peers(act):
        for k in sorted(range(1, ny), key=lambda k: -min(k, ny - k)):
            j = lax.rem(y + k, ny)
            act(j, (dp, j))

    def rep_peers(act):
        for k in sorted(range(1, nrep), key=lambda k: -min(k, nrep - k)):
            j = lax.rem(rep + k, nrep)
            act(j, (j * nb + b, y))

    def block_peers(act):
        for k in range(1, nb):
            j = lax.rem(b + k, nb)
            act(j, (rep * nb + j, y))

    def chip_peers(act):
        def at_z(i, carry):
            step = lax.div(i + 1, 2)
            to_z = lax.rem(z + nz // 2 + jnp.where(lax.rem(i, 2) == 1, nz - step, step), nz)
            for k in sorted(range(nx), key=lambda k: -min(k, nx - k)):
                j = to_z * nx + lax.rem(x + k, nx)
                if k == 0:
                    pl.when(j != chip)(functools.partial(act, j, (j * nc + c, y)))
                else:
                    act(j, (j * nc + c, y))
            return carry

        lax.fori_loop(0, nz, at_z, 0)

    barrier = pltpu.get_barrier_semaphore()

    def greet(device):
        pl.semaphore_signal(barrier, inc=1, device_id=device, device_id_type=MESH)

    chip_peers(lambda j, device: greet(device))
    y_peers(lambda j, device: greet(device))
    for k in range(nzl * nx):
        greet((rep * nb + lax.rem(b + nc * k, nb) + 1 - 2 * c, y))

    @pl.when(moved)
    def _():
        greet((l_dst, y))
        greet((l_src, y))

    greeted = chips - 1 + ny - 1 + nzl * nx

    def remote(src, dst, stage, it, device):
        return pltpu.make_async_remote_copy(
            src_ref=src, dst_ref=dst, send_sem=send_sem.at[stage, it], recv_sem=recv_sem.at[stage, it],
            device_id=device, device_id_type=MESH,
        )

    pending = []

    def swap(stage, it, peers, src, slots, me, count):
        peers(lambda j, device: remote(src(j), slots.at[me], stage, it, device).start())
        whole = remote(slots.at[:count], slots.at[:count], stage, it, partner)
        pending.append(whole.wait_send)
        return whole.wait_recv

    def total(slots, n):
        return functools.reduce(jnp.add, [slots[j] for j in range(n)])

    loads[0].wait()
    q_packed = jnp.concatenate([wv[:, :half], wv[:, half:]], axis=0).T
    loads[1].wait()
    loads[2].wait()
    cv[...] = (gv[...].astype(F32) + ev[...].astype(F32)).astype(BF16)
    low = lanes((half_rows, 128)) < RANK

    for it in range(ITERS):
        one = jnp.dot(cv[:, :half], q_packed, preferred_element_type=F32)
        two = jnp.dot(cv[:, half:], q_packed, preferred_element_type=F32)
        packed = jnp.where(
            low,
            one[:half_rows] + pltpu.roll(two[:half_rows], RANK, 1),
            pltpu.roll(one[half_rows:], RANK, 1) + two[half_rows:],
        )
        p_send[it] = packed.reshape(ny, half_rows // ny, 128)
        if it == 0:
            pl.semaphore_wait(barrier, greeted + jnp.where(moved, 2, 0))
        wait = swap(0, it, y_peers, lambda j: p_send.at[it, j], p_rs.at[it], y, ny - 1)
        p_rs[it, y] = p_send[it, y]
        if it == 0:
            ctv[...] = cv[...].T.reshape(ctv.shape)
        wait()
        p_z[it, rep] = total(p_rs.at[it], ny)
        swap(1, it, rep_peers, lambda j: p_z.at[it, rep], p_z.at[it], rep, nrep - 1)()
        p_ag[it, y] = total(p_z.at[it], nrep)
        swap(2, it, y_peers, lambda j: p_ag.at[it, y], p_ag.at[it], y, ny - 1)()
        p_whole = p_ag[it].reshape(half_rows, 128)

        first, second = spread(p_whole)
        terms = list(zip(split3(first), split3(second)))

        def right_term(core):
            result = None
            for one_p, two_p in terms:
                term = jnp.dot(ctv[0, core], one_p, preferred_element_type=F32)
                term += jnp.dot(ctv[1, core], two_p, preferred_element_type=F32)
                result = term if result is None else result + term
            return result

        q_send[it] = right_term(1 - c)
        half_copy = remote(q_send.at[it], q_core.at[it], 3, it, partner)
        half_copy.start()
        pending.append(half_copy.wait_send)

        gram2 = lax.dot_general(
            p_whole, p_whole, (((0,), (0,)), ((), ())), precision=HIGH, preferred_element_type=F32
        )
        gram = gram2[:RANK] + pltpu.roll(gram2[RANK:], RANK, 1)
        low_t = lanes((TILE, 128)) < RANK
        for h in range(nc):
            upper, lower = gram[2 * h * TILE : (2 * h + 1) * TILE], gram[(2 * h + 1) * TILE : (2 * h + 2) * TILE]
            g_send[it, h] = jnp.where(low_t, upper, pltpu.roll(lower, RANK, 1))
        g_x[it, b] = g_send[it, c]
        wait_gram = swap(4, it, block_peers, lambda j: g_send.at[it, lax.rem(j, nc)], g_x.at[it], b, nb - 1)

        own_half = right_term(c)
        half_copy.wait_recv()
        q_sum[it] = (own_half + q_core[it]).reshape(q_sum.shape[1:])

        def send_share(j, device):
            @pl.when(j < owners)
            def _():
                remote(q_sum.at[it, j], q_x.at[it, chip], 5, it, device).start()

        chip_peers(send_share)

        wait_gram()
        g_ag[it, c] = total(g_x.at[it], nb)
        own_gram, other_gram = g_ag.at[it, c], g_ag.at[it, 1 - c]
        gram_copy = remote(own_gram, own_gram, 6, it, partner)
        gram_copy.start()
        pending.append(gram_copy.wait_send)
        remote(other_gram, other_gram, 6, it, partner).wait_recv()
        pieces = []
        for h in range(nc):
            whole = g_ag[it, h]
            pieces += [whole, pltpu.roll(whole, RANK, 1)]
        lane = lanes((RANK, 128))
        unit = (lane - RANK == lax.broadcasted_iota(jnp.int32, (RANK, 128), 0)).astype(F32)
        eliminate(jnp.where(lane < RANK, jnp.concatenate(pieces, axis=0), unit), chol)
        inverse = chol[...]
        turned = pltpu.roll(inverse, RANK, 1)
        solve = jnp.concatenate([jnp.where(lane < RANK, turned, 0.0), jnp.where(lane < RANK, 0.0, inverse)], axis=0)

        @pl.when(chip < owners)
        def _():
            q_x[it, chip] = q_sum[it, chip]
            most = q_x.at[it, : chips - 1]
            remote(most, most, 5, it, partner).wait_recv()
            mine = q_ag.at[it, c, chip]
            mine[...] = (nt(jnp.sum(q_x[it], axis=0), solve) / nrep).astype(BF16)
            chip_peers(lambda j, device: remote(mine, mine, 7, it, device).start())

        if it == ITERS - 1:
            left = nt(p_whole, solve)
            turned_left = left.T
            per_half = nrep // 2
            wide = rows // nrep
            for r in range(nrep):
                h, o = r // per_half, r % per_half * wide
                l_send[r] = turned_left[h * RANK : (h + 1) * RANK, o : o + wide]
            l_copy = remote(l_send.at[rep], l_recv, 9, 0, (l_dst, y))

            @pl.when(moved)
            def _():
                l_copy.start()

            @pl.when(jnp.logical_not(moved))
            def _():
                l_recv[...] = l_send[rep]

            p_first, p_second = spread(left)
            p_first, p_second = p_first.astype(BF16), p_second.astype(BF16)

        @pl.when(chip < owners)
        def _():
            others = q_ag.at[it, c, : owners - 1]
            remote(others, others, 7, it, partner).wait_recv()

        @pl.when(chip >= owners)
        def _():
            others = q_ag.at[it, c]
            remote(others, others, 7, it, partner).wait_recv()

        all_copy = remote(q_ag.at[it, c], q_ag.at[it, c], 8, it, partner)
        all_copy.start()
        pending.append(all_copy.wait_send)
        other = q_ag.at[it, 1 - c]
        remote(other, other, 8, it, partner).wait_recv()
        q_packed = q_ag[it].reshape(half, 128)

    q_turned = q_packed.T
    right_ref[:, :half] = q_turned[:RANK]
    right_ref[:, half:] = q_turned[RANK:]
    stores = []
    for at_half, left_half in ((0, p_first), (half, p_second)):
        span = slice(at_half, at_half + half)
        rebuilt = jnp.dot(left_half, q_turned, preferred_element_type=F32)
        nev[:, span] = (gv[:, span].astype(F32) + ev[:, span].astype(F32) - rebuilt).astype(BF16)
        stores.append(pltpu.make_async_copy(nev.at[:, span], ne_hbm.at[:, span], store_sem.at[len(stores)]))
        stores[-1].start()

    @pl.when(moved)
    def _():
        l_copy.wait()

    left_ref[...] = l_recv[...]
    sized = size_ref.at[: chips - 1]
    for it in range(ITERS):

        @pl.when(chip < owners)
        def _():
            most = q_sum.at[it, : owners - 1]
            remote(most, most, 5, it, partner).wait_send()
            remote(sized, sized, 7, it, partner).wait_send()

        @pl.when(chip >= owners)
        def _():
            remote(q_sum.at[it], q_sum.at[it], 5, it, partner).wait_send()

    for done in pending:
        done()
    for store in stores:
        store.wait()


def step(geo, gradients, errors, warm_factor):
    nrep, nzl, nx, nc, ny = geo
    nb = nzl * nx * nc
    chips = nrep * nzl * nx
    rows, cols = gradients.shape
    half = cols // 2
    part = rows // 2 // ny
    core_rows = half // nc
    owners = core_rows // TILE
    stages = 10
    dma = pltpu.SemaphoreType.DMA
    vmem = pltpu.VMEM
    any_spec = pl.BlockSpec(memory_space=pl.ANY)
    vmem_spec = pl.BlockSpec(memory_space=pltpu.VMEM)
    return pl.pallas_call(
        functools.partial(kernel, geo),
        out_shape=(
            jax.ShapeDtypeStruct((rows, cols), BF16),
            jax.ShapeDtypeStruct((RANK, rows // nrep), F32),
            jax.ShapeDtypeStruct((RANK, cols), BF16),
        ),
        in_specs=[any_spec, any_spec, any_spec],
        out_specs=(any_spec, vmem_spec, vmem_spec),
        scratch_shapes=[
            vmem((rows, cols), BF16), vmem((rows, cols), BF16), vmem((RANK, cols), BF16), vmem((rows, cols), BF16),
            vmem((2, nc, core_rows, rows), BF16), vmem((rows, cols), BF16),
            vmem((ITERS, ny, part, 128), F32), vmem((ITERS, ny, part, 128), F32),
            vmem((ITERS, nrep, part, 128), F32), vmem((ITERS, ny, part, 128), F32),
            vmem((ITERS, nc, TILE, 128), F32), vmem((ITERS, nb, TILE, 128), F32),
            vmem((ITERS, nc, TILE, 128), F32), vmem((RANK, 128), F32),
            vmem((ITERS, core_rows, 128), F32), vmem((ITERS, core_rows, 128), F32),
            vmem((ITERS, owners, TILE, 128), F32), vmem((ITERS, chips, TILE, 128), F32),
            vmem((ITERS, nc, owners, TILE, 128), BF16), vmem((chips, TILE, 128), BF16),
            vmem((nrep, RANK, rows // nrep), F32), vmem((RANK, rows // nrep), F32),
            dma((3,)), dma((2,)), dma((stages, ITERS)), dma((stages, ITERS)),
        ],
        compiler_params=pltpu.CompilerParams(
            collective_id=0, has_side_effects=True, vmem_limit_bytes=60 * 1024 * 1024
        ),
        name="power_step",
    )(gradients, errors, warm_factor)


def build(mesh, geo):
    in_specs = (P("dp", "tensor"), P("dp", "tensor"), P(None, "tensor"))
    out_specs = (P("dp", "tensor"), P(None, "dp"), P(None, "tensor"))
    return jax.shard_map(
        functools.partial(step, geo), mesh=mesh, in_specs=in_specs, out_specs=out_specs, check_vma=False
    )


def solution(mesh):
    return build(mesh, (4, 2, 4, 2, 8))
```

```python
import functools

import jax
import jax.numpy as jnp
from jax import lax
from jax.experimental import pallas as pl
from jax.experimental.pallas import tpu as pltpu
from jax.sharding import PartitionSpec as P

ITERS = 2
MESH = pl.DeviceIdType.MESH
HIGH = lax.Precision.HIGHEST
F32 = jnp.float32
BF16 = jnp.bfloat16
RANK = 64
TILE = 16


def lanes(shape):
    return lax.broadcasted_iota(jnp.int32, shape, 1)


def spread(x):
    low = lanes(x.shape) < RANK
    turned = pltpu.roll(x, RANK, 1)
    zero = jnp.zeros_like(x)
    first = jnp.concatenate([jnp.where(low, x, zero), jnp.where(low, turned, zero)], axis=0)
    second = jnp.concatenate([jnp.where(low, zero, turned), jnp.where(low, zero, x)], axis=0)
    return first, second


def split2(x):
    hi = x.astype(BF16)
    return hi, (x - hi.astype(F32)).astype(BF16)


def nt(a, b):
    return lax.dot_general(a, b, (((1,), (1,)), ((), ())), precision=HIGH, preferred_element_type=F32)


def eliminate(rows, out_ref):
    block = 8
    for k0 in range(0, RANK, block):
        n = rows.shape[0]
        cols = [jnp.broadcast_to(rows[:, k0 + j : k0 + j + 1], (n, 128)) for j in range(block)]
        for i in range(block):
            pivot = cols[i][i : i + 1, :]
            row = rows[i : i + 1, :]
            out_ref[k0 + i : k0 + i + 1, :] = row * lax.rsqrt(pivot)
            if k0 + i == RANK - 1:
                break
            factor = cols[i] * (1.0 / pivot)
            rows = rows - factor * row
            for j in range(i + 1, block):
                cols[j] = cols[j] - factor * cols[j][i : i + 1, :]
        rows = rows[block:, :] if n > block else rows


def kernel(
    geo, g_hbm, e_hbm, w_hbm, ne_out, left_out, right_out,
    gv, ev, wv, cv, ctv, nev, rv,
    p_send, p_rs, p_z, p_ag, g_send, g_x, g_ag, chol,
    q_send, q_core, q_sum, q_x, q_ag, size_ref, l_send, l_recv,
    load_sem, store_sem, send_sem, recv_sem, piece_send, piece_recv,
):
    nrep, nzl, nx, nc, ny = geo
    nb = nzl * nx * nc
    nz = nrep * nzl
    chips = nz * nx
    owners = q_ag.shape[2]
    share = owners // nrep
    dp, y = lax.axis_index("dp"), lax.axis_index("tensor")
    c = lax.rem(dp, nc)
    b = lax.rem(dp, nb)
    rep = lax.div(dp, nb)
    chip = lax.div(dp, nc)
    x = lax.rem(chip, nx)
    z = lax.div(chip, nx)
    at_rep = lax.div(b, nc)
    owns = at_rep < share
    mine_at = rep * share + at_rep
    rows, cols = gv.shape
    half_rows, half = rows // 2, cols // 2
    partner = (dp + 1 - 2 * c, y)
    l_dst = nrep * b + rep
    l_src = lax.rem(dp, nrep) * nb + lax.div(dp, nrep)
    moved = l_dst != dp

    parts = [pl.ds(h * half_rows, half_rows) for h in range(2)]
    pairs = [(w_hbm, wv)] + [(src.at[part], dst.at[part]) for part in parts for src, dst in ((g_hbm, gv), (e_hbm, ev))]
    loads = [pltpu.make_async_copy(src, dst, load_sem.at[i]) for i, (src, dst) in enumerate(pairs)]
    for load in loads:
        load.start()

    def y_peers(act):
        for k in sorted(range(1, ny), key=lambda k: -min(k, ny - k)):
            j = lax.rem(y + k, ny)
            act(j, (dp, j))

    def rep_peers(act):
        for k in sorted(range(1, nrep), key=lambda k: -min(k, nrep - k)):
            j = lax.rem(rep + k, nrep)
            act(j, (j * nb + b, y))

    def block_peers(act):
        for k in range(1, nb):
            j = lax.rem(b + k, nb)
            act(j, (rep * nb + j, y))

    def chip_peers(act):
        def at_z(i, carry):
            step = lax.div(i + 1, 2)
            to_z = lax.rem(z + nz // 2 + jnp.where(lax.rem(i, 2) == 1, nz - step, step), nz)
            for k in sorted(range(nx), key=lambda k: -min(k, nx - k)):
                j = to_z * nx + lax.rem(x + k, nx)
                if k == 0:
                    pl.when(j != chip)(functools.partial(act, j, (j * nc + c, y)))
                else:
                    act(j, (j * nc + c, y))
            return carry

        lax.fori_loop(0, nz, at_z, 0)

    barrier = pltpu.get_barrier_semaphore()

    def greet(device):
        pl.semaphore_signal(barrier, inc=1, device_id=device, device_id_type=MESH)

    chip_peers(lambda j, device: greet(device))
    y_peers(lambda j, device: greet(device))
    for k in range(nzl * nx):
        greet((rep * nb + lax.rem(b + nc * k, nb) + 1 - 2 * c, y))

    @pl.when(moved)
    def _():
        greet((l_dst, y))
        greet((l_src, y))

    greeted = chips - 1 + ny - 1 + nzl * nx

    def remote(src, dst, stage, it, device):
        return pltpu.make_async_remote_copy(
            src_ref=src, dst_ref=dst, send_sem=send_sem.at[stage, it], recv_sem=recv_sem.at[stage, it],
            device_id=device, device_id_type=MESH,
        )

    pending = []

    def swap(stage, it, peers, src, slots, me, count):
        peers(lambda j, device: remote(src(j), slots.at[me], stage, it, device).start())
        whole = remote(slots.at[:count], slots.at[:count], stage, it, partner)
        pending.append(whole.wait_send)
        return whole.wait_recv

    def total(slots, n):
        return functools.reduce(jnp.add, [slots[j] for j in range(n)])

    loads[0].wait()
    q_packed = jnp.concatenate([wv[:, :half], wv[:, half:]], axis=0).T
    low = lanes((half_rows, 128)) < RANK

    for it in range(ITERS):
        ones, twos = [], []
        for h, part in enumerate(parts):
            if it == 0:
                loads[1 + 2 * h].wait()
                loads[2 + 2 * h].wait()
                cv[part] = (gv[part].astype(F32) + ev[part].astype(F32)).astype(BF16)
            ones.append(jnp.dot(cv[part, :half], q_packed, preferred_element_type=F32))
            twos.append(jnp.dot(cv[part, half:], q_packed, preferred_element_type=F32))
        packed = jnp.where(low, ones[0] + pltpu.roll(twos[0], RANK, 1), pltpu.roll(ones[1], RANK, 1) + twos[1])
        p_send[it] = packed.reshape(ny, half_rows // ny, 128)
        if it == 0:
            pl.semaphore_wait(barrier, greeted + jnp.where(moved, 2, 0))
        wait = swap(0, it, y_peers, lambda j: p_send.at[it, j], p_rs.at[it], y, ny - 1)
        p_rs[it, y] = p_send[it, y]
        if it == 0:
            ctv[...] = cv[...].T.reshape(ctv.shape)
        wait()
        p_z[it, rep] = total(p_rs.at[it], ny)
        swap(1, it, rep_peers, lambda j: p_z.at[it, rep], p_z.at[it], rep, nrep - 1)()
        p_ag[it, y] = total(p_z.at[it], nrep)
        swap(2, it, y_peers, lambda j: p_ag.at[it, y], p_ag.at[it], y, ny - 1)()
        p_whole = p_ag[it].reshape(half_rows, 128)

        first, second = spread(p_whole)
        terms = list(zip(split2(first), split2(second)))

        def right_term(core, group):
            result = None
            for one_p, two_p in terms:
                term = jnp.dot(ctv[0, core, group], one_p, preferred_element_type=F32)
                term += jnp.dot(ctv[1, core, group], two_p, preferred_element_type=F32)
                result = term if result is None else result + term
            return result

        groups = [lax.rem(rep + k, nrep) for k in sorted(range(nrep), key=lambda k: -min(k, nrep - k))]
        pieces = []
        for i, group in enumerate(groups):
            q_send[it, i] = right_term(1 - c, group)
            pieces.append(
                pltpu.make_async_remote_copy(
                    src_ref=q_send.at[it, i], dst_ref=q_core.at[it, i], send_sem=piece_send.at[it, i],
                    recv_sem=piece_recv.at[it, i], device_id=partner, device_id_type=MESH,
                )
            )
            pieces[-1].start()
            pending.append(pieces[-1].wait_send)

        gram2 = lax.dot_general(
            p_whole, p_whole, (((0,), (0,)), ((), ())), precision=HIGH, preferred_element_type=F32
        )
        gram = gram2[:RANK] + pltpu.roll(gram2[RANK:], RANK, 1)
        low_t = lanes((TILE, 128)) < RANK
        for h in range(nc):
            upper, lower = gram[2 * h * TILE : (2 * h + 1) * TILE], gram[(2 * h + 1) * TILE : (2 * h + 2) * TILE]
            g_send[it, h] = jnp.where(low_t, upper, pltpu.roll(lower, RANK, 1))
        g_x[it, b] = g_send[it, c]
        wait_gram = swap(4, it, block_peers, lambda j: g_send.at[it, lax.rem(j, nc)], g_x.at[it], b, nb - 1)

        for i, group in enumerate(groups):
            own = right_term(c, group)
            pieces[i].wait_recv()
            q_sum[it, pl.ds(group * share, share)] = (own + q_core[it, i]).reshape(share, TILE, 128)
            for k in range(share):
                j = group * (nb // nc) + k

                @pl.when(j != chip)
                def _(j=j, k=k, group=group):
                    remote(q_sum.at[it, group * share + k], q_x.at[it, chip], 5, it, (j * nc + c, y)).start()

        wait_gram()
        g_ag[it, c] = total(g_x.at[it], nb)
        own_gram, other_gram = g_ag.at[it, c], g_ag.at[it, 1 - c]
        gram_copy = remote(own_gram, own_gram, 6, it, partner)
        gram_copy.start()
        pending.append(gram_copy.wait_send)
        remote(other_gram, other_gram, 6, it, partner).wait_recv()
        blocks = []
        for h in range(nc):
            whole = g_ag[it, h]
            blocks += [whole, pltpu.roll(whole, RANK, 1)]
        lane = lanes((RANK, 128))
        unit = (lane - RANK == lax.broadcasted_iota(jnp.int32, (RANK, 128), 0)).astype(F32)
        eliminate(jnp.where(lane < RANK, jnp.concatenate(blocks, axis=0), unit), chol)
        inverse = chol[...]
        turned = pltpu.roll(inverse, RANK, 1)
        solve = jnp.concatenate([jnp.where(lane < RANK, turned, 0.0), jnp.where(lane < RANK, 0.0, inverse)], axis=0)

        @pl.when(owns)
        def _():
            q_x[it, chip] = q_sum[it, mine_at]
            most = q_x.at[it, : chips - 1]
            remote(most, most, 5, it, partner).wait_recv()
            mine = q_ag.at[it, c, mine_at]
            mine[...] = (nt(jnp.sum(q_x[it], axis=0), solve) / nrep).astype(BF16)
            chip_peers(lambda j, device: remote(mine, mine, 7, it, device).start())

        if it == ITERS - 1:
            left = nt(p_whole, solve)
            turned_left = left.T
            per_half = nrep // 2
            wide = rows // nrep
            for r in range(nrep):
                h, o = r // per_half, r % per_half * wide
                l_send[r] = turned_left[h * RANK : (h + 1) * RANK, o : o + wide]
            l_copy = remote(l_send.at[rep], l_recv, 9, 0, (l_dst, y))

            @pl.when(moved)
            def _():
                l_copy.start()

            @pl.when(jnp.logical_not(moved))
            def _():
                l_recv[...] = l_send[rep]

            p_first, p_second = spread(left)
            p_first, p_second = p_first.astype(BF16), p_second.astype(BF16)

        @pl.when(owns)
        def _():
            others = q_ag.at[it, c, : owners - 1]
            remote(others, others, 7, it, partner).wait_recv()

        @pl.when(jnp.logical_not(owns))
        def _():
            others = q_ag.at[it, c]
            remote(others, others, 7, it, partner).wait_recv()

        all_copy = remote(q_ag.at[it, c], q_ag.at[it, c], 8, it, partner)
        all_copy.start()
        pending.append(all_copy.wait_send)
        other = q_ag.at[it, 1 - c]
        remote(other, other, 8, it, partner).wait_recv()
        q_packed = q_ag[it].reshape(half, 128)

    q_turned = q_packed.T
    rv[:, :half] = q_turned[:RANK]
    rv[:, half:] = q_turned[RANK:]
    stores = [pltpu.make_async_copy(rv, right_out, store_sem.at[0])]
    stores[0].start()
    for at_half, left_half in ((0, p_first), (half, p_second)):
        span = pl.ds(at_half, half)
        rebuilt = jnp.dot(left_half, q_turned, preferred_element_type=F32)
        nev[:, span] = (gv[:, span].astype(F32) + ev[:, span].astype(F32) - rebuilt).astype(BF16)
        stores.append(pltpu.make_async_copy(nev.at[:, span], ne_out.at[:, span], store_sem.at[len(stores)]))
        stores[-1].start()

    @pl.when(moved)
    def _():
        l_copy.wait()

    stores.append(pltpu.make_async_copy(l_recv, left_out, store_sem.at[len(stores)]))
    stores[-1].start()
    sized = size_ref.at[: chips - 1]
    for it in range(ITERS):

        @pl.when(owns)
        def _():
            most = q_sum.at[it, : owners - 1]
            remote(most, most, 5, it, partner).wait_send()
            remote(sized, sized, 7, it, partner).wait_send()

        @pl.when(jnp.logical_not(owns))
        def _():
            remote(q_sum.at[it], q_sum.at[it], 5, it, partner).wait_send()

    for done in pending:
        done()
    for store in stores:
        store.wait()


def place(*refs):
    n = (len(refs) - 1) // 2
    copies = [pltpu.make_async_copy(refs[i], refs[n + i], refs[-1].at[i]) for i in range(n)]
    for copy in copies:
        copy.start()
    for copy in copies:
        copy.wait()


def step(geo, gradients, errors, warm_factor):
    nrep, nzl, nx, nc, ny = geo
    nb = nzl * nx * nc
    chips = nrep * nzl * nx
    rows, cols = gradients.shape
    half = cols // 2
    part = rows // 2 // ny
    core_rows = half // nc
    piece = core_rows // nrep
    owners = core_rows // TILE
    stages = 10
    dma = pltpu.SemaphoreType.DMA
    vmem = pltpu.VMEM
    any_spec = pl.BlockSpec(memory_space=pl.ANY)
    hbm_spec = pl.BlockSpec(memory_space=pltpu.HBM)
    out_shape = (
        jax.ShapeDtypeStruct((rows, cols), BF16),
        jax.ShapeDtypeStruct((RANK, rows // nrep), F32),
        jax.ShapeDtypeStruct((RANK, cols), BF16),
    )
    results = pl.pallas_call(
        functools.partial(kernel, geo),
        out_shape=out_shape,
        in_specs=[hbm_spec] * 3,
        out_specs=(any_spec,) * 3,
        scratch_shapes=[
            vmem((rows, cols), BF16), vmem((rows, cols), BF16), vmem((RANK, cols), BF16), vmem((rows, cols), BF16),
            vmem((2, nc, nrep, piece, rows), BF16), vmem((rows, cols), BF16), vmem((RANK, cols), BF16),
            vmem((ITERS, ny, part, 128), F32), vmem((ITERS, ny, part, 128), F32),
            vmem((ITERS, nrep, part, 128), F32), vmem((ITERS, ny, part, 128), F32),
            vmem((ITERS, nc, TILE, 128), F32), vmem((ITERS, nb, TILE, 128), F32),
            vmem((ITERS, nc, TILE, 128), F32), vmem((RANK, 128), F32),
            vmem((ITERS, nrep, piece, 128), F32), vmem((ITERS, nrep, piece, 128), F32),
            vmem((ITERS, owners, TILE, 128), F32), vmem((ITERS, chips, TILE, 128), F32),
            vmem((ITERS, nc, owners, TILE, 128), BF16), vmem((chips, TILE, 128), BF16),
            vmem((nrep, RANK, rows // nrep), F32), vmem((RANK, rows // nrep), F32),
            dma((5,)), dma((4,)), dma((stages, ITERS)), dma((stages, ITERS)), dma((ITERS, nrep)), dma((ITERS, nrep)),
        ],
        compiler_params=pltpu.CompilerParams(
            collective_id=0, has_side_effects=True, vmem_limit_bytes=52 * 1024 * 1024
        ),
        name="power_step",
    )(gradients, errors, warm_factor)
    return pl.pallas_call(
        place,
        out_shape=out_shape,
        in_specs=[any_spec] * 3,
        out_specs=(any_spec,) * 3,
        scratch_shapes=[dma((3,))],
        compiler_params=pltpu.CompilerParams(vmem_limit_bytes=8 * 1024 * 1024),
        name="place",
    )(*results)


def build(mesh, geo):
    in_specs = (P("dp", "tensor"), P("dp", "tensor"), P(None, "tensor"))
    out_specs = (P("dp", "tensor"), P(None, "dp"), P(None, "tensor"))
    return jax.shard_map(
        functools.partial(step, geo), mesh=mesh, in_specs=in_specs, out_specs=out_specs, check_vma=False
    )


def solution(mesh):
    return build(mesh, (4, 2, 4, 2, 8))
```

```python
import functools

import jax
import jax.numpy as jnp
from jax import lax
from jax.experimental import pallas as pl
from jax.experimental.pallas import tpu as pltpu
from jax.sharding import PartitionSpec as P

ITERS = 2
MESH = pl.DeviceIdType.MESH
HIGH = lax.Precision.HIGHEST
F32 = jnp.float32
BF16 = jnp.bfloat16
RANK = 64
TILE = 16


def lanes(shape):
    return lax.broadcasted_iota(jnp.int32, shape, 1)


def spread(x):
    low = lanes(x.shape) < RANK
    turned = pltpu.roll(x, RANK, 1)
    zero = jnp.zeros_like(x)
    first = jnp.concatenate([jnp.where(low, x, zero), jnp.where(low, turned, zero)], axis=0)
    second = jnp.concatenate([jnp.where(low, zero, turned), jnp.where(low, zero, x)], axis=0)
    return first, second


def split2(x):
    hi = x.astype(BF16)
    return hi, (x - hi.astype(F32)).astype(BF16)


def nt(a, b):
    return lax.dot_general(a, b, (((1,), (1,)), ((), ())), precision=HIGH, preferred_element_type=F32)


def eliminate(rows, out_ref):
    block = 8
    for k0 in range(0, RANK, block):
        n = rows.shape[0]
        cols = [jnp.broadcast_to(rows[:, k0 + j : k0 + j + 1], (n, 128)) for j in range(block)]
        for i in range(block):
            pivot = cols[i][i : i + 1, :]
            row = rows[i : i + 1, :]
            out_ref[k0 + i : k0 + i + 1, :] = row * lax.rsqrt(pivot)
            if k0 + i == RANK - 1:
                break
            factor = cols[i] * (1.0 / pivot)
            rows = rows - factor * row
            for j in range(i + 1, block):
                cols[j] = cols[j] - factor * cols[j][i : i + 1, :]
        rows = rows[block:, :] if n > block else rows


def kernel(
    geo, g_hbm, e_hbm, w_hbm, ne_out, left_out, right_out,
    gv, ev, wv, cv, ctv, nev, rv,
    p_send, p_rs, p_own, p_far, p_near, p_n, g_send, g_x, g_ag, chol,
    q_send, q_core, q_sum, q_x, q_ag, size_ref, l_send, l_recv,
    load_sem, store_sem, send_sem, recv_sem, piece_send, piece_recv,
):
    nrep, nzl, nx, nc, ny = geo
    nb = nzl * nx * nc
    nz = nrep * nzl
    chips = nz * nx
    owners = q_ag.shape[2]
    share = owners // nrep
    dp, y = lax.axis_index("dp"), lax.axis_index("tensor")
    c = lax.rem(dp, nc)
    b = lax.rem(dp, nb)
    rep = lax.div(dp, nb)
    chip = lax.div(dp, nc)
    x = lax.rem(chip, nx)
    z = lax.div(chip, nx)
    at_rep = lax.div(b, nc)
    owns = at_rep < share
    mine_at = rep * share + at_rep
    rows, cols = gv.shape
    half_rows, half = rows // 2, cols // 2
    partner = (dp + 1 - 2 * c, y)
    l_dst = nrep * b + rep
    moved = l_dst != dp

    parts = [pl.ds(h * half_rows, half_rows) for h in range(2)]
    pairs = [(w_hbm, wv)] + [(src.at[part], dst.at[part]) for part in parts for src, dst in ((g_hbm, gv), (e_hbm, ev))]
    loads = [pltpu.make_async_copy(src, dst, load_sem.at[i]) for i, (src, dst) in enumerate(pairs)]
    for load in loads:
        load.start()

    def y_peers(act):
        for k in sorted(range(1, ny), key=lambda k: -min(k, ny - k)):
            j = lax.rem(y + k, ny)
            act(j, (dp, j))

    def far_peers(act):
        far = lax.rem(rep + nrep // 2, nrep) * nb + b
        for k in sorted(range(ny), key=lambda k: -min(k, ny - k)):
            j = lax.rem(y + k, ny)
            act(j, (far, j))

    def near_device(step):
        return (lax.rem(rep + nrep + step, nrep) * nb + b, y)

    def block_peers(act):
        for k in range(1, nb):
            j = lax.rem(b + k, nb)
            act(j, (rep * nb + j, y))

    def chip_peers(act):
        def at_z(i, carry):
            step = lax.div(i + 1, 2)
            to_z = lax.rem(z + nz // 2 + jnp.where(lax.rem(i, 2) == 1, nz - step, step), nz)
            for k in sorted(range(nx), key=lambda k: -min(k, nx - k)):
                j = to_z * nx + lax.rem(x + k, nx)
                if k == 0:
                    pl.when(j != chip)(functools.partial(act, j, (j * nc + c, y)))
                else:
                    act(j, (j * nc + c, y))
            return carry

        lax.fori_loop(0, nz, at_z, 0)

    barrier = pltpu.get_barrier_semaphore()

    def greet(device):
        pl.semaphore_signal(barrier, inc=1, device_id=device, device_id_type=MESH)

    y_peers(lambda j, device: greet(device))
    for k in range(1, nrep):
        greet((lax.rem(rep + k, nrep) * nb + b, y))
    block_peers(lambda j, device: greet(device))
    greeted = ny - 1 + nrep - 1 + nb - 1

    def remote(src, dst, stage, it, device):
        return pltpu.make_async_remote_copy(
            src_ref=src, dst_ref=dst, send_sem=send_sem.at[stage, it], recv_sem=recv_sem.at[stage, it],
            device_id=device, device_id_type=MESH,
        )

    pending = []

    def swap(stage, it, peers, src, slots, me, count):
        peers(lambda j, device: remote(src(j), slots.at[me], stage, it, device).start())
        whole = remote(slots.at[:count], slots.at[:count], stage, it, partner)
        pending.append(whole.wait_send)
        return whole.wait_recv

    def total(slots, n):
        return functools.reduce(jnp.add, [slots[j] for j in range(n)])

    loads[0].wait()
    q_packed = jnp.concatenate([wv[:, :half], wv[:, half:]], axis=0).T
    low = lanes((half_rows, 128)) < RANK

    for it in range(ITERS):
        ones, twos = [], []
        for h, part in enumerate(parts):
            if it == 0:
                loads[1 + 2 * h].wait()
                loads[2 + 2 * h].wait()
                cv[part] = (gv[part].astype(F32) + ev[part].astype(F32)).astype(BF16)
            ones.append(jnp.dot(cv[part, :half], q_packed, preferred_element_type=F32))
            twos.append(jnp.dot(cv[part, half:], q_packed, preferred_element_type=F32))
        packed = jnp.where(low, ones[0] + pltpu.roll(twos[0], RANK, 1), pltpu.roll(ones[1], RANK, 1) + twos[1])
        p_send[it] = packed.reshape(ny, half_rows // ny, 128)
        if it == 0:
            pl.semaphore_wait(barrier, greeted)
        wait = swap(0, it, y_peers, lambda j: p_send.at[it, j], p_rs.at[it], y, ny - 1)
        p_rs[it, y] = p_send[it, y]
        if it == 0:
            ctv[...] = cv[...].T.reshape(ctv.shape)
        wait()
        mine = p_own.at[it, y]
        mine[...] = total(p_rs.at[it], ny)
        for slot, step in ((1, 1), (0, -1)):
            remote(mine, p_near.at[it, slot], 1, it, near_device(step)).start()
        both = remote(p_near.at[it], p_near.at[it], 1, it, partner)
        pending.append(both.wait_send)
        wait_far = swap(2, it, far_peers, lambda j: mine, p_far.at[it], y, ny)
        wait_own = swap(3, it, y_peers, lambda j: mine, p_own.at[it], y, ny - 1)
        both.wait_recv()
        p_n[it, y] = p_near[it, 0] + p_near[it, 1]
        wait_near = swap(9, it, y_peers, lambda j: p_n.at[it, y], p_n.at[it], y, ny - 1)
        wait_own()
        wait_far()
        wait_near()
        p_whole = ((p_own[it] + p_far[it]) + p_n[it]).reshape(half_rows, 128)

        first, second = spread(p_whole)
        terms = list(zip(split2(first), split2(second)))

        def right_term(core, group):
            result = None
            for one_p, two_p in terms:
                term = jnp.dot(ctv[0, core, group], one_p, preferred_element_type=F32)
                term += jnp.dot(ctv[1, core, group], two_p, preferred_element_type=F32)
                result = term if result is None else result + term
            return result

        groups = [lax.rem(rep + k, nrep) for k in sorted(range(nrep), key=lambda k: -min(k, nrep - k))]
        pieces = []
        for i, group in enumerate(groups):
            q_send[it, i] = right_term(1 - c, group)
            pieces.append(
                pltpu.make_async_remote_copy(
                    src_ref=q_send.at[it, i], dst_ref=q_core.at[it, i], send_sem=piece_send.at[it, i],
                    recv_sem=piece_recv.at[it, i], device_id=partner, device_id_type=MESH,
                )
            )
            pieces[-1].start()
            pending.append(pieces[-1].wait_send)

        gram2 = lax.dot_general(
            p_whole, p_whole, (((0,), (0,)), ((), ())), precision=HIGH, preferred_element_type=F32
        )
        gram = gram2[:RANK] + pltpu.roll(gram2[RANK:], RANK, 1)
        low_t = lanes((TILE, 128)) < RANK
        for h in range(nc):
            upper, lower = gram[2 * h * TILE : (2 * h + 1) * TILE], gram[(2 * h + 1) * TILE : (2 * h + 2) * TILE]
            g_send[it, h] = jnp.where(low_t, upper, pltpu.roll(lower, RANK, 1))
        g_x[it, b] = g_send[it, c]
        wait_gram = swap(4, it, block_peers, lambda j: g_send.at[it, lax.rem(j, nc)], g_x.at[it], b, nb - 1)

        for i, group in enumerate(groups):
            own = right_term(c, group)
            pieces[i].wait_recv()
            q_sum[it, pl.ds(group * share, share)] = (own + q_core[it, i]).reshape(share, TILE, 128)
            for k in range(share):
                j = group * (nb // nc) + k

                @pl.when(j != chip)
                def _(j=j, k=k, group=group):
                    remote(q_sum.at[it, group * share + k], q_x.at[it, chip], 5, it, (j * nc + c, y)).start()

        wait_gram()
        g_ag[it, c] = total(g_x.at[it], nb)
        own_gram, other_gram = g_ag.at[it, c], g_ag.at[it, 1 - c]
        gram_copy = remote(own_gram, own_gram, 6, it, partner)
        gram_copy.start()
        pending.append(gram_copy.wait_send)
        remote(other_gram, other_gram, 6, it, partner).wait_recv()
        blocks = []
        for h in range(nc):
            whole = g_ag[it, h]
            blocks += [whole, pltpu.roll(whole, RANK, 1)]
        lane = lanes((RANK, 128))
        unit = (lane - RANK == lax.broadcasted_iota(jnp.int32, (RANK, 128), 0)).astype(F32)
        eliminate(jnp.where(lane < RANK, jnp.concatenate(blocks, axis=0), unit), chol)
        inverse = chol[...]
        turned = pltpu.roll(inverse, RANK, 1)
        solve = jnp.concatenate([jnp.where(lane < RANK, turned, 0.0), jnp.where(lane < RANK, 0.0, inverse)], axis=0)

        @pl.when(owns)
        def _():
            q_x[it, chip] = q_sum[it, mine_at]
            most = q_x.at[it, : chips - 1]
            remote(most, most, 5, it, partner).wait_recv()
            mine = q_ag.at[it, c, mine_at]
            mine[...] = (nt(jnp.sum(q_x[it], axis=0), solve) / nrep).astype(BF16)
            chip_peers(lambda j, device: remote(mine, mine, 7, it, device).start())

        if it == ITERS - 1:
            left = nt(p_whole, solve)
            turned_left = left.T
            per_half = nrep // 2
            wide = rows // nrep
            for r in range(nrep):
                h, o = r // per_half, r % per_half * wide
                l_send[r] = turned_left[h * RANK : (h + 1) * RANK, o : o + wide]
            l_copy = remote(l_send.at[rep], l_recv, 10, 0, (l_dst, y))

            @pl.when(moved)
            def _():
                l_copy.start()

            @pl.when(jnp.logical_not(moved))
            def _():
                l_recv[...] = l_send[rep]

            p_first, p_second = spread(left)
            p_first, p_second = p_first.astype(BF16), p_second.astype(BF16)

        @pl.when(owns)
        def _():
            others = q_ag.at[it, c, : owners - 1]
            remote(others, others, 7, it, partner).wait_recv()

        @pl.when(jnp.logical_not(owns))
        def _():
            others = q_ag.at[it, c]
            remote(others, others, 7, it, partner).wait_recv()

        all_copy = remote(q_ag.at[it, c], q_ag.at[it, c], 8, it, partner)
        all_copy.start()
        pending.append(all_copy.wait_send)
        other = q_ag.at[it, 1 - c]
        remote(other, other, 8, it, partner).wait_recv()
        q_packed = q_ag[it].reshape(half, 128)

    q_turned = q_packed.T
    rv[:, :half] = q_turned[:RANK]
    rv[:, half:] = q_turned[RANK:]
    stores = [pltpu.make_async_copy(rv, right_out, store_sem.at[0])]
    stores[0].start()
    for at_half, left_half in ((0, p_first), (half, p_second)):
        span = pl.ds(at_half, half)
        rebuilt = jnp.dot(left_half, q_turned, preferred_element_type=F32)
        nev[:, span] = (gv[:, span].astype(F32) + ev[:, span].astype(F32) - rebuilt).astype(BF16)
        stores.append(pltpu.make_async_copy(nev.at[:, span], ne_out.at[:, span], store_sem.at[len(stores)]))
        stores[-1].start()

    @pl.when(moved)
    def _():
        l_copy.wait()

    stores.append(pltpu.make_async_copy(l_recv, left_out, store_sem.at[len(stores)]))
    stores[-1].start()
    sized = size_ref.at[: chips - 1]
    for it in range(ITERS):

        @pl.when(owns)
        def _():
            most = q_sum.at[it, : owners - 1]
            remote(most, most, 5, it, partner).wait_send()
            remote(sized, sized, 7, it, partner).wait_send()

        @pl.when(jnp.logical_not(owns))
        def _():
            remote(q_sum.at[it], q_sum.at[it], 5, it, partner).wait_send()

    for done in pending:
        done()
    for store in stores:
        store.wait()


def place(*refs):
    n = (len(refs) - 1) // 2
    copies = [pltpu.make_async_copy(refs[i], refs[n + i], refs[-1].at[i]) for i in range(n)]
    for copy in copies:
        copy.start()
    for copy in copies:
        copy.wait()


def step(geo, gradients, errors, warm_factor):
    nrep, nzl, nx, nc, ny = geo
    nb = nzl * nx * nc
    chips = nrep * nzl * nx
    rows, cols = gradients.shape
    half = cols // 2
    part = rows // 2 // ny
    core_rows = half // nc
    piece = core_rows // nrep
    owners = core_rows // TILE
    stages = 11
    dma = pltpu.SemaphoreType.DMA
    vmem = pltpu.VMEM
    any_spec = pl.BlockSpec(memory_space=pl.ANY)
    hbm_spec = pl.BlockSpec(memory_space=pltpu.HBM)
    out_shape = (
        jax.ShapeDtypeStruct((rows, cols), BF16),
        jax.ShapeDtypeStruct((RANK, rows // nrep), F32),
        jax.ShapeDtypeStruct((RANK, cols), BF16),
    )
    results = pl.pallas_call(
        functools.partial(kernel, geo),
        out_shape=out_shape,
        in_specs=[hbm_spec] * 3,
        out_specs=(any_spec,) * 3,
        scratch_shapes=[
            vmem((rows, cols), BF16), vmem((rows, cols), BF16), vmem((RANK, cols), BF16), vmem((rows, cols), BF16),
            vmem((2, nc, nrep, piece, rows), BF16), vmem((rows, cols), BF16), vmem((RANK, cols), BF16),
            vmem((ITERS, ny, part, 128), F32), vmem((ITERS, ny, part, 128), F32),
            vmem((ITERS, ny, part, 128), F32), vmem((ITERS, ny, part, 128), F32),
            vmem((ITERS, 2, part, 128), F32), vmem((ITERS, ny, part, 128), F32),
            vmem((ITERS, nc, TILE, 128), F32), vmem((ITERS, nb, TILE, 128), F32),
            vmem((ITERS, nc, TILE, 128), F32), vmem((RANK, 128), F32),
            vmem((ITERS, nrep, piece, 128), F32), vmem((ITERS, nrep, piece, 128), F32),
            vmem((ITERS, owners, TILE, 128), F32), vmem((ITERS, chips, TILE, 128), F32),
            vmem((ITERS, nc, owners, TILE, 128), BF16), vmem((chips, TILE, 128), BF16),
            vmem((nrep, RANK, rows // nrep), F32), vmem((RANK, rows // nrep), F32),
            dma((5,)), dma((4,)), dma((stages, ITERS)), dma((stages, ITERS)), dma((ITERS, nrep)), dma((ITERS, nrep)),
        ],
        compiler_params=pltpu.CompilerParams(
            collective_id=0, has_side_effects=True, vmem_limit_bytes=52 * 1024 * 1024
        ),
        name="power_step",
    )(gradients, errors, warm_factor)
    return pl.pallas_call(
        place,
        out_shape=out_shape,
        in_specs=[any_spec] * 3,
        out_specs=(any_spec,) * 3,
        scratch_shapes=[dma((3,))],
        compiler_params=pltpu.CompilerParams(vmem_limit_bytes=8 * 1024 * 1024),
        name="place",
    )(*results)


def build(mesh, geo):
    in_specs = (P("dp", "tensor"), P("dp", "tensor"), P(None, "tensor"))
    out_specs = (P("dp", "tensor"), P(None, "dp"), P(None, "tensor"))
    return jax.shard_map(
        functools.partial(step, geo), mesh=mesh, in_specs=in_specs, out_specs=out_specs, check_vma=False
    )


def solution(mesh):
    return build(mesh, (4, 2, 4, 2, 8))
```

```python
import functools

import jax
import jax.numpy as jnp
from jax import lax
from jax.experimental import pallas as pl
from jax.experimental.pallas import tpu as pltpu
from jax.sharding import PartitionSpec as P

ITERS = 2
MESH = pl.DeviceIdType.MESH
HIGH = lax.Precision.HIGHEST
F32 = jnp.float32
BF16 = jnp.bfloat16
RANK = 64
TILE = 16


def lanes(shape):
    return lax.broadcasted_iota(jnp.int32, shape, 1)


def spread(x):
    low = lanes(x.shape) < RANK
    turned = pltpu.roll(x, RANK, 1)
    zero = jnp.zeros_like(x)
    first = jnp.concatenate([jnp.where(low, x, zero), jnp.where(low, turned, zero)], axis=0)
    second = jnp.concatenate([jnp.where(low, zero, turned), jnp.where(low, zero, x)], axis=0)
    return first, second


def split2(x):
    hi = x.astype(BF16)
    return hi, (x - hi.astype(F32)).astype(BF16)


def split3(x):
    hi, rest = split2(x)
    mid = rest
    return hi, mid, (x - hi.astype(F32) - mid.astype(F32)).astype(BF16)


def six_left(x):
    hi, mid, lo = split3(x)
    return jnp.concatenate([hi, hi, mid, hi, lo, mid], axis=1)


def six_right(x):
    hi, mid, lo = split3(x)
    return jnp.concatenate([hi, mid, hi, lo, hi, mid], axis=0)


def eliminate(rows, out_ref):
    block = 8
    for k0 in range(0, RANK, block):
        n = rows.shape[0]
        cols = [jnp.broadcast_to(rows[:, k0 + j : k0 + j + 1], (n, 128)) for j in range(block)]
        for i in range(block):
            pivot = cols[i][i : i + 1, :]
            row = rows[i : i + 1, :]
            out_ref[k0 + i : k0 + i + 1, :] = row * lax.rsqrt(pivot)
            if k0 + i == RANK - 1:
                break
            factor = cols[i] * (1.0 / pivot)
            rows = rows - factor * row
            for j in range(i + 1, block):
                cols[j] = cols[j] - factor * cols[j][i : i + 1, :]
        rows = rows[block:, :] if n > block else rows


def kernel(
    geo, g_hbm, e_hbm, w_hbm, ne0, ne1, ne2, ne3, ne4, ne5, left_out, right_out,
    gv, ev, wv, cv, cs, ctv, nev, rv,
    p_send, p_rs, p_own, p_far, p_near, p_n, g_send, g_x, g_ag, chol, solver,
    q_send, q_core, q_sum, q_x, q_ag, size_ref, l_send, l_recv,
    load_sem, store_sem, send_sem, recv_sem, piece_send, piece_recv,
):
    ne_outs = (ne0, ne1, ne2, ne3, ne4, ne5)
    nrep, nzl, nx, nc, ny = geo
    nb = nzl * nx * nc
    nz = nrep * nzl
    chips = nz * nx
    owners = q_ag.shape[2]
    share = owners // nrep
    dp, y = lax.axis_index("dp"), lax.axis_index("tensor")
    c = lax.rem(dp, nc)
    b = lax.rem(dp, nb)
    rep = lax.div(dp, nb)
    chip = lax.div(dp, nc)
    x = lax.rem(chip, nx)
    z = lax.div(chip, nx)
    at_rep = lax.div(b, nc)
    owns = at_rep < share
    mine_at = rep * share + at_rep
    rows, cols = gv.shape
    half_rows, half = rows // 2, cols // 2
    partner = (dp + 1 - 2 * c, y)
    l_dst = nrep * b + rep
    moved = l_dst != dp

    def y_peers(act):
        for k in sorted(range(1, ny), key=lambda k: -min(k, ny - k)):
            j = lax.rem(y + k, ny)
            act(j, (dp, j))

    def far_peers(act):
        far = lax.rem(rep + nrep // 2, nrep) * nb + b
        for k in sorted(range(ny), key=lambda k: -min(k, ny - k)):
            j = lax.rem(y + k, ny)
            act(j, (far, j))

    def near_device(step):
        return (lax.rem(rep + nrep + step, nrep) * nb + b, y)

    def block_peers(act):
        for k in range(1, nb):
            j = lax.rem(b + k, nb)
            act(j, (rep * nb + j, y))

    def chip_peers(act):
        def at_z(i, carry):
            step = lax.div(i + 1, 2)
            to_z = lax.rem(z + nz // 2 + jnp.where(lax.rem(i, 2) == 1, nz - step, step), nz)
            for k in sorted(range(nx), key=lambda k: -min(k, nx - k)):
                j = to_z * nx + lax.rem(x + k, nx)
                if k == 0:
                    pl.when(j != chip)(functools.partial(act, j, (j * nc + c, y)))
                else:
                    act(j, (j * nc + c, y))
            return carry

        lax.fori_loop(0, nz, at_z, 0)

    barrier = pltpu.get_barrier_semaphore()

    def greet(device):
        pl.semaphore_signal(barrier, inc=1, device_id=device, device_id_type=MESH)

    y_peers(lambda j, device: greet(device))
    for k in range(1, nrep):
        greet((lax.rem(rep + k, nrep) * nb + b, y))
    block_peers(lambda j, device: greet(device))
    greeted = ny - 1 + nrep - 1 + nb - 1
    parts = [pl.ds(h * (rows // 4), rows // 4) for h in range(4)]
    pairs = [(w_hbm, wv)] + [(src.at[part], dst.at[part]) for part in parts for src, dst in ((g_hbm, gv), (e_hbm, ev))]
    loads = [pltpu.make_async_copy(src, dst, load_sem.at[i]) for i, (src, dst) in enumerate(pairs)]
    for load in loads:
        load.start()

    def remote(src, dst, stage, it, device):
        return pltpu.make_async_remote_copy(
            src_ref=src, dst_ref=dst, send_sem=send_sem.at[stage, it], recv_sem=recv_sem.at[stage, it],
            device_id=device, device_id_type=MESH,
        )

    pending = []

    def swap(stage, it, peers, src, slots, me, count):
        peers(lambda j, device: remote(src(j), slots.at[me], stage, it, device).start())
        whole = remote(slots.at[:count], slots.at[:count], stage, it, partner)
        pending.append(whole.wait_send)
        return whole.wait_recv

    def total(slots, n):
        return functools.reduce(jnp.add, [slots[j] for j in range(n)])

    loads[0].wait()
    q_packed = jnp.concatenate([wv[:, :half], wv[:, half:]], axis=0).T
    low = lanes((half_rows, 128)) < RANK

    for it in range(ITERS):
        if it == 0:
            ones, twos = [], []
            for h, part in enumerate(parts):
                loads[1 + 2 * h].wait()
                loads[2 + 2 * h].wait()
                cv[part] = (gv[part].astype(F32) + ev[part].astype(F32)).astype(BF16)
                ones.append(jnp.dot(cv[part, :half], q_packed, preferred_element_type=F32))
                twos.append(jnp.dot(cv[part, half:], q_packed, preferred_element_type=F32))
            one, two = jnp.concatenate(ones, axis=0), jnp.concatenate(twos, axis=0)
            packed = jnp.where(
                low,
                one[:half_rows] + pltpu.roll(two[:half_rows], RANK, 1),
                pltpu.roll(one[half_rows:], RANK, 1) + two[half_rows:],
            )
            one, two = jnp.concatenate(ones, axis=0), jnp.concatenate(twos, axis=0)
        else:
            own_q = q_ag[it - 1, c].reshape(half // nc, 128)
            one = jnp.dot(cs[0, c], own_q, preferred_element_type=F32)
            two = jnp.dot(cs[1, c], own_q, preferred_element_type=F32)
            wait_other()
            other_q = q_ag[it - 1, 1 - c].reshape(half // nc, 128)
            one += jnp.dot(cs[0, 1 - c], other_q, preferred_element_type=F32)
            two += jnp.dot(cs[1, 1 - c], other_q, preferred_element_type=F32)
        packed = jnp.where(
            low,
            one[:half_rows] + pltpu.roll(two[:half_rows], RANK, 1),
            pltpu.roll(one[half_rows:], RANK, 1) + two[half_rows:],
        )
        p_send[it] = packed.reshape(ny, half_rows // ny, 128)
        if it == 0:
            pl.semaphore_wait(barrier, greeted)
        wait = swap(0, it, y_peers, lambda j: p_send.at[it, j], p_rs.at[it], y, ny - 1)
        p_rs[it, y] = p_send[it, y]
        if it == 0:
            ctv[...] = cv[...].T.reshape(ctv.shape)
            for i in range(2 * nc):
                cs[i // nc, i % nc] = cv[:, i * (half // nc) : (i + 1) * (half // nc)]
        wait()
        mine = p_own.at[it]
        mine[...] = total(p_rs.at[it], ny)
        for slot, step in ((1, 1), (0, -1)):
            remote(mine, p_near.at[it, slot], 1, it, near_device(step)).start()
        both = remote(p_near.at[it], p_near.at[it], 1, it, partner)
        pending.append(both.wait_send)
        wait_far = swap(2, it, far_peers, lambda j: mine, p_far.at[it], y, ny)
        both.wait_recv()
        p_n[it, y] = p_own[it] + (p_near[it, 0] + p_near[it, 1])
        wait_near = swap(9, it, y_peers, lambda j: p_n.at[it, y], p_n.at[it], y, ny - 1)
        wait_far()
        wait_near()
        p_whole = (p_far[it] + p_n[it]).reshape(half_rows, 128)

        first, second = spread(p_whole)
        terms = list(zip(split2(first), split2(second)))

        def right_term(core, group):
            result = None
            for one_p, two_p in terms:
                term = jnp.dot(ctv[0, core, group], one_p, preferred_element_type=F32)
                term += jnp.dot(ctv[1, core, group], two_p, preferred_element_type=F32)
                result = term if result is None else result + term
            return result

        groups = [lax.rem(rep + k, nrep) for k in sorted(range(nrep), key=lambda k: -min(k, nrep - k))]
        pieces = []
        for i, group in enumerate(groups):
            q_send[it, i] = right_term(1 - c, group)
            pieces.append(
                pltpu.make_async_remote_copy(
                    src_ref=q_send.at[it, i], dst_ref=q_core.at[it, i], send_sem=piece_send.at[it, i],
                    recv_sem=piece_recv.at[it, i], device_id=partner, device_id_type=MESH,
                )
            )
            pieces[-1].start()
            pending.append(pieces[-1].wait_send)

        gram2 = lax.dot_general(
            p_whole, p_whole, (((0,), (0,)), ((), ())), precision=HIGH, preferred_element_type=F32
        )
        gram = gram2[:RANK] + pltpu.roll(gram2[RANK:], RANK, 1)
        low_t = lanes((TILE, 128)) < RANK
        for h in range(nc):
            upper, lower = gram[2 * h * TILE : (2 * h + 1) * TILE], gram[(2 * h + 1) * TILE : (2 * h + 2) * TILE]
            g_send[it, h] = jnp.where(low_t, upper, pltpu.roll(lower, RANK, 1))
        g_x[it, b] = g_send[it, c]
        wait_gram = swap(4, it, block_peers, lambda j: g_send.at[it, lax.rem(j, nc)], g_x.at[it], b, nb - 1)

        for i, group in enumerate(groups):
            own = right_term(c, group)
            pieces[i].wait_recv()
            q_sum[it, pl.ds(group * share, share)] = (own + q_core[it, i]).reshape(share, TILE, 128)
            for k in range(share):
                j = group * (nb // nc) + k

                @pl.when(j != chip)
                def _(j=j, k=k, group=group):
                    remote(q_sum.at[it, group * share + k], q_x.at[it, chip], 5, it, (j * nc + c, y)).start()

        wait_gram()
        g_ag[it, c] = total(g_x.at[it], nb)
        own_gram, other_gram = g_ag.at[it, c], g_ag.at[it, 1 - c]
        gram_copy = remote(own_gram, own_gram, 6, it, partner)
        gram_copy.start()
        pending.append(gram_copy.wait_send)
        remote(other_gram, other_gram, 6, it, partner).wait_recv()
        blocks = []
        for h in range(nc):
            whole = g_ag[it, h]
            blocks += [whole, pltpu.roll(whole, RANK, 1)]
        lane = lanes((RANK, 128))
        unit = (lane - RANK == lax.broadcasted_iota(jnp.int32, (RANK, 128), 0)).astype(F32)
        eliminate(jnp.where(lane < RANK, jnp.concatenate(blocks, axis=0), unit), chol)
        inverse = chol[...]
        turned = pltpu.roll(inverse, RANK, 1)
        solve = jnp.concatenate([jnp.where(lane < RANK, turned, 0.0), jnp.where(lane < RANK, 0.0, inverse)], axis=0)
        solver[...] = six_right(solve.T)

        def solved(x):
            return jnp.dot(six_left(x), solver[...], preferred_element_type=F32)

        @pl.when(owns)
        def _():
            q_x[it, chip] = q_sum[it, mine_at]
            most = q_x.at[it, : chips - 1]
            remote(most, most, 5, it, partner).wait_recv()
            mine = q_ag.at[it, c, mine_at]
            mine[...] = (solved(jnp.sum(q_x[it], axis=0)) / nrep).astype(BF16)
            chip_peers(lambda j, device: remote(mine, mine, 7, it, device).start())

        if it == ITERS - 1:
            left = solved(p_whole)
            turned_left = left.T
            per_half = nrep // 2
            wide = rows // nrep
            for r in range(nrep):
                h, o = r // per_half, r % per_half * wide
                l_send[r] = turned_left[h * RANK : (h + 1) * RANK, o : o + wide]
            l_copy = remote(l_send.at[rep], l_recv, 10, 0, (l_dst, y))

            @pl.when(moved)
            def _():
                l_copy.start()

            @pl.when(jnp.logical_not(moved))
            def _():
                l_recv[...] = l_send[rep]

            p_first, p_second = spread(left)
            p_first, p_second = p_first.astype(BF16), p_second.astype(BF16)

        @pl.when(owns)
        def _():
            others = q_ag.at[it, c, : owners - 1]
            remote(others, others, 7, it, partner).wait_recv()

        @pl.when(jnp.logical_not(owns))
        def _():
            others = q_ag.at[it, c]
            remote(others, others, 7, it, partner).wait_recv()

        all_copy = remote(q_ag.at[it, c], q_ag.at[it, c], 8, it, partner)
        all_copy.start()
        pending.append(all_copy.wait_send)
        other = q_ag.at[it, 1 - c]
        wait_other = remote(other, other, 8, it, partner).wait_recv

    wait_other()
    q_turned = q_ag[ITERS - 1].reshape(half, 128).T
    rv[:, :half] = q_turned[:RANK]
    rv[:, half:] = q_turned[RANK:]
    stores = [pltpu.make_async_copy(rv, right_out, store_sem.at[0])]
    stores[0].start()
    per_half = len(ne_outs) // 2
    at = 0
    for h, left_half in enumerate((p_first, p_second)):
        span = pl.ds(h * half, half)
        rebuilt = jnp.dot(left_half, q_turned, preferred_element_type=F32)
        nev[:, span] = (gv[:, span].astype(F32) + ev[:, span].astype(F32) - rebuilt).astype(BF16)
        for ne_out in ne_outs[h * per_half : (h + 1) * per_half]:
            wide = ne_out.shape[1]
            stores.append(pltpu.make_async_copy(nev.at[:, pl.ds(at, wide)], ne_out, store_sem.at[len(stores)]))
            stores[-1].start()
            at += wide

    @pl.when(moved)
    def _():
        l_copy.wait()

    stores.append(pltpu.make_async_copy(l_recv, left_out, store_sem.at[len(stores)]))
    stores[-1].start()
    sized = size_ref.at[: chips - 1]
    for it in range(ITERS):

        @pl.when(owns)
        def _():
            most = q_sum.at[it, : owners - 1]
            remote(most, most, 5, it, partner).wait_send()
            remote(sized, sized, 7, it, partner).wait_send()

        @pl.when(jnp.logical_not(owns))
        def _():
            remote(q_sum.at[it], q_sum.at[it], 5, it, partner).wait_send()

    for done in pending:
        done()
    for store in stores:
        store.wait()


def place(*refs):
    *sources, new_errors, left, right, sem = refs
    pieces, targets, at = sources[:-2], [], 0
    for piece in pieces:
        targets.append(new_errors.at[:, pl.ds(at, piece.shape[1])])
        at += piece.shape[1]
    targets += [left, right]
    copies = [pltpu.make_async_copy(src, dst, sem.at[i]) for i, (src, dst) in enumerate(zip(sources, targets))]
    for copy in copies:
        copy.start()
    for copy in copies:
        copy.wait()


def step(geo, gradients, errors, warm_factor):
    nrep, nzl, nx, nc, ny = geo
    nb = nzl * nx * nc
    chips = nrep * nzl * nx
    rows, cols = gradients.shape
    half = cols // 2
    part = rows // 2 // ny
    core_rows = half // nc
    piece = core_rows // nrep
    owners = core_rows // TILE
    stages = 11
    dma = pltpu.SemaphoreType.DMA
    vmem = pltpu.VMEM
    any_spec = pl.BlockSpec(memory_space=pl.ANY)
    hbm_spec = pl.BlockSpec(memory_space=pltpu.HBM)
    out_shape = (
        jax.ShapeDtypeStruct((rows, cols), BF16),
        jax.ShapeDtypeStruct((RANK, rows // nrep), F32),
        jax.ShapeDtypeStruct((RANK, cols), BF16),
    )
    unit = half // 7
    widths = (2 * unit, 2 * unit, 3 * unit) * 2
    results = pl.pallas_call(
        functools.partial(kernel, geo),
        out_shape=tuple(jax.ShapeDtypeStruct((rows, wide), BF16) for wide in widths) + out_shape[1:],
        in_specs=[hbm_spec] * 3,
        out_specs=(any_spec,) * 8,
        scratch_shapes=[
            vmem((rows, cols), BF16), vmem((rows, cols), BF16), vmem((RANK, cols), BF16), vmem((rows, cols), BF16),
            vmem((2, nc, rows, core_rows), BF16), vmem((2, nc, nrep, piece, rows), BF16), vmem((rows, cols), BF16), vmem((RANK, cols), BF16),
            vmem((ITERS, ny, part, 128), F32), vmem((ITERS, ny, part, 128), F32),
            vmem((ITERS, part, 128), F32), vmem((ITERS, ny, part, 128), F32),
            vmem((ITERS, 2, part, 128), F32), vmem((ITERS, ny, part, 128), F32),
            vmem((ITERS, nc, TILE, 128), F32), vmem((ITERS, nb, TILE, 128), F32),
            vmem((ITERS, nc, TILE, 128), F32), vmem((RANK, 128), F32), vmem((6 * 128, 128), BF16),
            vmem((ITERS, nrep, piece, 128), F32), vmem((ITERS, nrep, piece, 128), F32),
            vmem((ITERS, owners, TILE, 128), F32), vmem((ITERS, chips, TILE, 128), F32),
            vmem((ITERS, nc, owners, TILE, 128), BF16), vmem((chips, TILE, 128), BF16),
            vmem((nrep, RANK, rows // nrep), F32), vmem((RANK, rows // nrep), F32),
            dma((9,)), dma((8,)), dma((stages, ITERS)), dma((stages, ITERS)), dma((ITERS, nrep)), dma((ITERS, nrep)),
        ],
        compiler_params=pltpu.CompilerParams(
            collective_id=0, has_side_effects=True, vmem_limit_bytes=(52 * 1024 + 640) * 1024
        ),
        name="power_step",
    )(gradients, errors, warm_factor)
    return pl.pallas_call(
        place,
        out_shape=out_shape,
        in_specs=[any_spec] * 8,
        out_specs=(any_spec,) * 3,
        scratch_shapes=[dma((8,))],
        compiler_params=pltpu.CompilerParams(vmem_limit_bytes=8 * 1024 * 1024),
        name="place",
    )(*results)


def build(mesh, geo):
    in_specs = (P("dp", "tensor"), P("dp", "tensor"), P(None, "tensor"))
    out_specs = (P("dp", "tensor"), P(None, "dp"), P(None, "tensor"))
    return jax.shard_map(
        functools.partial(step, geo), mesh=mesh, in_specs=in_specs, out_specs=out_specs, check_vma=False
    )


def solution(mesh):
    return build(mesh, (4, 2, 4, 2, 8))
```

```python
import functools

import jax
import jax.numpy as jnp
from jax import lax
from jax.experimental import pallas as pl
from jax.experimental.pallas import tpu as pltpu
from jax.sharding import PartitionSpec as P

ITERS = 2
MESH = pl.DeviceIdType.MESH
HIGH = lax.Precision.HIGHEST
F32 = jnp.float32
BF16 = jnp.bfloat16
RANK = 64
TILE = 16


def lanes(shape):
    return lax.broadcasted_iota(jnp.int32, shape, 1)


def spread(x):
    low = lanes(x.shape) < RANK
    turned = pltpu.roll(x, RANK, 1)
    zero = jnp.zeros_like(x)
    first = jnp.concatenate([jnp.where(low, x, zero), jnp.where(low, turned, zero)], axis=0)
    second = jnp.concatenate([jnp.where(low, zero, turned), jnp.where(low, zero, x)], axis=0)
    return first, second


def split2(x):
    hi = x.astype(BF16)
    return hi, (x - hi.astype(F32)).astype(BF16)


def split3(x):
    hi, rest = split2(x)
    mid = rest
    return hi, mid, (x - hi.astype(F32) - mid.astype(F32)).astype(BF16)


def six_left(x):
    hi, mid, lo = split3(x)
    return jnp.concatenate([hi, hi, mid, hi, lo, mid], axis=1)


def six_right(x):
    hi, mid, lo = split3(x)
    return jnp.concatenate([hi, mid, hi, lo, hi, mid], axis=0)


def eliminate(rows, out_ref):
    block = 16
    for k0 in range(0, RANK, block):
        n = rows.shape[0]
        cols = [jnp.broadcast_to(rows[:, k0 + j : k0 + j + 1], (n, 128)) for j in range(block)]
        for i in range(block):
            scale = lax.rsqrt(cols[i][i : i + 1, :])
            row = rows[i : i + 1, :] * scale
            out_ref[k0 + i : k0 + i + 1, :] = row
            if k0 + i == RANK - 1:
                break
            factor = cols[i] * scale
            rows = rows - factor * row
            for j in range(i + 1, block):
                cols[j] = cols[j] - factor * (cols[j][i : i + 1, :] * scale)
        rows = rows[block:, :] if n > block else rows


def kernel(
    geo, g_hbm, e_hbm, w_hbm, ne0, ne1, ne2, ne3, ne4, ne5, left_out, right_out,
    gv, ev, wv, cv, cs, ctv, nev, rv, qt,
    p_send, p_rs, p_own, p_far, p_near, p_n, g_send, g_x, g_ag, chol, solver,
    q_send, q_core, q_sum, q_x, q_ag, size_ref, l_send, l_recv,
    load_sem, store_sem, send_sem, recv_sem, piece_send, piece_recv,
):
    ne_outs = (ne0, ne1, ne2, ne3, ne4, ne5)
    nrep, nzl, nx, nc, ny = geo
    nb = nzl * nx * nc
    nz = nrep * nzl
    chips = nz * nx
    owners = q_ag.shape[2]
    share = owners // nrep
    dp, y = lax.axis_index("dp"), lax.axis_index("tensor")
    c = lax.rem(dp, nc)
    b = lax.rem(dp, nb)
    rep = lax.div(dp, nb)
    chip = lax.div(dp, nc)
    x = lax.rem(chip, nx)
    z = lax.div(chip, nx)
    at_rep = lax.div(b, nc)
    owns = at_rep < share
    mine_at = rep * share + at_rep
    rows, cols = gv.shape
    half_rows, half = rows // 2, cols // 2
    partner = (dp + 1 - 2 * c, y)
    l_dst = nrep * b + rep
    moved = l_dst != dp

    def y_peers(act):
        for k in sorted(range(1, ny), key=lambda k: -min(k, ny - k)):
            j = lax.rem(y + k, ny)
            act(j, (dp, j))

    def far_peers(act):
        far = lax.rem(rep + nrep // 2, nrep) * nb + b
        for k in sorted(range(ny), key=lambda k: -min(k, ny - k)):
            j = lax.rem(y + k, ny)
            act(j, (far, j))

    def near_device(step):
        return (lax.rem(rep + nrep + step, nrep) * nb + b, y)

    def block_peers(act):
        for k in range(1, nb):
            j = lax.rem(b + k, nb)
            act(j, (rep * nb + j, y))

    def chip_peers(act):
        def at_z(i, carry):
            step = lax.div(i + 1, 2)
            to_z = lax.rem(z + nz // 2 + jnp.where(lax.rem(i, 2) == 1, nz - step, step), nz)
            for k in sorted(range(nx), key=lambda k: -min(k, nx - k)):
                j = to_z * nx + lax.rem(x + k, nx)
                if k == 0:
                    pl.when(j != chip)(functools.partial(act, j, (j * nc + c, y)))
                else:
                    act(j, (j * nc + c, y))
            return carry

        lax.fori_loop(0, nz, at_z, 0)

    barrier = pltpu.get_barrier_semaphore()

    def greet(device):
        pl.semaphore_signal(barrier, inc=1, device_id=device, device_id_type=MESH)

    y_peers(lambda j, device: greet(device))
    for k in range(1, nrep):
        greet((lax.rem(rep + k, nrep) * nb + b, y))
    block_peers(lambda j, device: greet(device))
    greeted = ny - 1 + nrep - 1 + nb - 1
    parts = [pl.ds(h * (rows // 4), rows // 4) for h in range(4)]
    pairs = [(w_hbm, wv)] + [(src.at[part], dst.at[part]) for part in parts for src, dst in ((g_hbm, gv), (e_hbm, ev))]
    loads = [pltpu.make_async_copy(src, dst, load_sem.at[i]) for i, (src, dst) in enumerate(pairs)]
    for load in loads:
        load.start()

    def remote(src, dst, stage, it, device):
        return pltpu.make_async_remote_copy(
            src_ref=src, dst_ref=dst, send_sem=send_sem.at[stage, it], recv_sem=recv_sem.at[stage, it],
            device_id=device, device_id_type=MESH,
        )

    pending = []

    def swap(stage, it, peers, src, slots, me, count):
        peers(lambda j, device: remote(src(j), slots.at[me], stage, it, device).start())
        whole = remote(slots.at[:count], slots.at[:count], stage, it, partner)
        pending.append(whole.wait_send)
        return whole.wait_recv

    def total(slots, n):
        return functools.reduce(jnp.add, [slots[j] for j in range(n)])

    loads[0].wait()
    q_packed = jnp.concatenate([wv[:, :half], wv[:, half:]], axis=0).T
    low = lanes((half_rows, 128)) < RANK

    for it in range(ITERS):
        if it == 0:
            ones, twos = [], []
            for h, part in enumerate(parts):
                loads[1 + 2 * h].wait()
                loads[2 + 2 * h].wait()
                cv[part] = (gv[part].astype(F32) + ev[part].astype(F32)).astype(BF16)
                ones.append(jnp.dot(cv[part, :half], q_packed, preferred_element_type=F32))
                twos.append(jnp.dot(cv[part, half:], q_packed, preferred_element_type=F32))
            one, two = jnp.concatenate(ones, axis=0), jnp.concatenate(twos, axis=0)
            packed = jnp.where(
                low,
                one[:half_rows] + pltpu.roll(two[:half_rows], RANK, 1),
                pltpu.roll(one[half_rows:], RANK, 1) + two[half_rows:],
            )
            one, two = jnp.concatenate(ones, axis=0), jnp.concatenate(twos, axis=0)
        else:
            own_q = q_ag[it - 1, c].reshape(half // nc, 128)
            one = jnp.dot(cs[0, c], own_q, preferred_element_type=F32)
            two = jnp.dot(cs[1, c], own_q, preferred_element_type=F32)
            wait_other()
            other_q = q_ag[it - 1, 1 - c].reshape(half // nc, 128)
            one += jnp.dot(cs[0, 1 - c], other_q, preferred_element_type=F32)
            two += jnp.dot(cs[1, 1 - c], other_q, preferred_element_type=F32)
        packed = jnp.where(
            low,
            one[:half_rows] + pltpu.roll(two[:half_rows], RANK, 1),
            pltpu.roll(one[half_rows:], RANK, 1) + two[half_rows:],
        )
        p_send[it] = packed.reshape(ny, half_rows // ny, 128)
        if it == 0:
            pl.semaphore_wait(barrier, greeted)
        wait = swap(0, it, y_peers, lambda j: p_send.at[it, j], p_rs.at[it], y, ny - 1)
        p_rs[it, y] = p_send[it, y]
        if it == 0:
            turned_c = cv[...].T.reshape(2, nc, nrep, -1, rows)
            for core in range(nc):
                for group in range(nrep):
                    ctv[core, group] = jnp.concatenate([turned_c[0, core, group], turned_c[1, core, group]], axis=1)
            for i in range(2 * nc):
                cs[i // nc, i % nc] = cv[:, i * (half // nc) : (i + 1) * (half // nc)]
        wait()
        mine = p_own.at[it]
        mine[...] = total(p_rs.at[it], ny)
        for slot, step in ((1, 1), (0, -1)):
            remote(mine, p_near.at[it, slot], 1, it, near_device(step)).start()
        both = remote(p_near.at[it], p_near.at[it], 1, it, partner)
        pending.append(both.wait_send)
        wait_far = swap(2, it, far_peers, lambda j: mine, p_far.at[it], y, ny)
        both.wait_recv()
        p_n[it, y] = p_own[it] + (p_near[it, 0] + p_near[it, 1])
        wait_near = swap(9, it, y_peers, lambda j: p_n.at[it, y], p_n.at[it], y, ny - 1)
        wait_far()
        wait_near()
        p_whole = (p_far[it] + p_n[it]).reshape(half_rows, 128)

        first, second = spread(p_whole)
        parts_of_p = jnp.concatenate(split2(jnp.concatenate([first, second], axis=0)), axis=1)

        def right_term(core, group):
            both = jnp.dot(ctv[core, group], parts_of_p, preferred_element_type=F32)
            return both[:, :128] + both[:, 128:]

        groups = [lax.rem(rep + k, nrep) for k in sorted(range(nrep), key=lambda k: -min(k, nrep - k))]
        pieces = []
        for i, group in enumerate(groups):
            q_send[it, i] = right_term(1 - c, group)
            pieces.append(
                pltpu.make_async_remote_copy(
                    src_ref=q_send.at[it, i], dst_ref=q_core.at[it, i], send_sem=piece_send.at[it, i],
                    recv_sem=piece_recv.at[it, i], device_id=partner, device_id_type=MESH,
                )
            )
            pieces[-1].start()
            pending.append(pieces[-1].wait_send)

        gram2 = lax.dot_general(
            p_whole, p_whole, (((0,), (0,)), ((), ())), precision=HIGH, preferred_element_type=F32
        )
        gram = gram2[:RANK] + pltpu.roll(gram2[RANK:], RANK, 1)
        low_t = lanes((TILE, 128)) < RANK
        for h in range(nc):
            upper, lower = gram[2 * h * TILE : (2 * h + 1) * TILE], gram[(2 * h + 1) * TILE : (2 * h + 2) * TILE]
            g_send[it, h] = jnp.where(low_t, upper, pltpu.roll(lower, RANK, 1))
        g_x[it, b] = g_send[it, c]
        wait_gram = swap(4, it, block_peers, lambda j: g_send.at[it, lax.rem(j, nc)], g_x.at[it], b, nb - 1)

        for i, group in enumerate(groups):
            own = right_term(c, group)
            pieces[i].wait_recv()
            q_sum[it, pl.ds(group * share, share)] = (own + q_core[it, i]).reshape(share, TILE, 128)
            for k in range(share):
                j = group * (nb // nc) + k

                @pl.when(j != chip)
                def _(j=j, k=k, group=group):
                    remote(q_sum.at[it, group * share + k], q_x.at[it, chip], 5, it, (j * nc + c, y)).start()

        wait_gram()
        g_ag[it, c] = total(g_x.at[it], nb)
        own_gram, other_gram = g_ag.at[it, c], g_ag.at[it, 1 - c]
        gram_copy = remote(own_gram, own_gram, 6, it, partner)
        gram_copy.start()
        pending.append(gram_copy.wait_send)
        remote(other_gram, other_gram, 6, it, partner).wait_recv()
        blocks = []
        for h in range(nc):
            whole = g_ag[it, h]
            blocks += [whole, pltpu.roll(whole, RANK, 1)]
        lane = lanes((RANK, 128))
        unit = (lane - RANK == lax.broadcasted_iota(jnp.int32, (RANK, 128), 0)).astype(F32)
        eliminate(jnp.where(lane < RANK, jnp.concatenate(blocks, axis=0), unit), chol)
        inverse = chol[...]
        turned = pltpu.roll(inverse, RANK, 1)
        solve = jnp.concatenate([jnp.where(lane < RANK, turned, 0.0), jnp.where(lane < RANK, 0.0, inverse)], axis=0)
        solver[...] = six_right(solve.T)

        def solved(x):
            return jnp.dot(six_left(x), solver[...], preferred_element_type=F32)

        @pl.when(owns)
        def _():
            q_x[it, chip] = q_sum[it, mine_at]
            most = q_x.at[it, : chips - 1]
            remote(most, most, 5, it, partner).wait_recv()
            mine = q_ag.at[it, c, mine_at]
            mine[...] = (solved(jnp.sum(q_x[it], axis=0)) / nrep).astype(BF16)
            for group in groups:
                stage = 11 if group is groups[0] else 7
                for k in range(nb // nc):
                    j = group * (nb // nc) + k

                    def send(j=j, stage=stage):
                        remote(mine, mine, stage, it, (j * nc + c, y)).start()

                    if group is groups[-1]:
                        pl.when(j != chip)(send)
                    else:
                        send()

        if it == ITERS - 1:
            left = solved(p_whole)
            turned_left = left.T
            per_half = nrep // 2
            wide = rows // nrep
            for r in range(nrep):
                h, o = r // per_half, r % per_half * wide
                l_send[r] = turned_left[h * RANK : (h + 1) * RANK, o : o + wide]
            l_copy = remote(l_send.at[rep], l_recv, 10, 0, (l_dst, y))

            @pl.when(moved)
            def _():
                l_copy.start()

            @pl.when(jnp.logical_not(moved))
            def _():
                l_recv[...] = l_send[rep]

            p_first, p_second = spread(left)
            p_first, p_second = p_first.astype(BF16), p_second.astype(BF16)

        most = size_ref.at[: (nrep - 1) * share]

        @pl.when(owns)
        def _():
            others = size_ref.at[: (nrep - 1) * share - 1]
            remote(others, others, 7, it, partner).wait_recv()

        @pl.when(jnp.logical_not(owns))
        def _():
            remote(most, most, 7, it, partner).wait_recv()

        for group in groups[1:] + groups[:1]:
            slab = q_ag.at[it, c, pl.ds(group * share, share)]
            passed = remote(slab, slab, 8, it, partner)
            if group is groups[0]:
                remote(slab, slab, 11, it, partner).wait_recv()
            passed.start()
        passed = remote(q_ag.at[it, c], q_ag.at[it, c], 8, it, partner)
        pending.append(passed.wait_send)
        wait_other = passed.wait_recv

    early = half // nc // 128 * 128
    late = half - early
    halves = ((0, p_first), (half, p_second))

    def renew(at, wide, q_part):
        for start, left_half in halves:
            span = pl.ds(pl.multiple_of(start + at, 128), wide)
            rebuilt = jnp.dot(left_half, q_part, preferred_element_type=F32)
            nev[:, span] = (gv[:, span].astype(F32) + ev[:, span].astype(F32) - rebuilt).astype(BF16)
            yield

    ahead = q_ag[ITERS - 1, c, pl.ds(c * ((late - half // nc) // TILE), early // TILE)]
    for _ in renew(c * late, early, ahead.reshape(early, 128).T):
        pass
    wait_other()
    q_turned = q_ag[ITERS - 1].reshape(half, 128).T
    qt[...] = q_turned
    rv[:, :half] = q_turned[:RANK]
    rv[:, half:] = q_turned[RANK:]
    stores = [pltpu.make_async_copy(rv, right_out, store_sem.at[0])]
    stores[0].start()
    per_half = len(ne_outs) // 2
    at = 0
    late_at = pl.multiple_of((1 - c) * early, 128)
    for h, _ in enumerate(renew(late_at, late, qt[:, pl.ds(late_at, late)])):
        for ne_out in ne_outs[h * per_half : (h + 1) * per_half]:
            wide = ne_out.shape[1]
            stores.append(pltpu.make_async_copy(nev.at[:, pl.ds(at, wide)], ne_out, store_sem.at[len(stores)]))
            stores[-1].start()
            at += wide

    @pl.when(moved)
    def _():
        l_copy.wait()

    stores.append(pltpu.make_async_copy(l_recv, left_out, store_sem.at[len(stores)]))
    stores[-1].start()
    sized = size_ref.at[: (nrep - 1) * (nb // nc) - 1]
    far_sized = size_ref.at[: nb // nc]
    for it in range(ITERS):

        @pl.when(owns)
        def _():
            most = q_sum.at[it, : owners - 1]
            remote(most, most, 5, it, partner).wait_send()
            remote(sized, sized, 7, it, partner).wait_send()
            remote(far_sized, far_sized, 11, it, partner).wait_send()

        @pl.when(jnp.logical_not(owns))
        def _():
            remote(q_sum.at[it], q_sum.at[it], 5, it, partner).wait_send()

    for done in pending:
        done()
    for store in stores:
        store.wait()


def place(*refs):
    *sources, new_errors, left, right, sem = refs
    pieces, targets, at = sources[:-2], [], 0
    for piece in pieces:
        targets.append(new_errors.at[:, pl.ds(at, piece.shape[1])])
        at += piece.shape[1]
    targets += [left, right]
    copies = [pltpu.make_async_copy(src, dst, sem.at[i]) for i, (src, dst) in enumerate(zip(sources, targets))]
    for copy in copies:
        copy.start()
    for copy in copies:
        copy.wait()


def step(geo, gradients, errors, warm_factor):
    nrep, nzl, nx, nc, ny = geo
    nb = nzl * nx * nc
    chips = nrep * nzl * nx
    rows, cols = gradients.shape
    half = cols // 2
    part = rows // 2 // ny
    core_rows = half // nc
    piece = core_rows // nrep
    owners = core_rows // TILE
    stages = 12
    dma = pltpu.SemaphoreType.DMA
    vmem = pltpu.VMEM
    any_spec = pl.BlockSpec(memory_space=pl.ANY)
    hbm_spec = pl.BlockSpec(memory_space=pltpu.HBM)
    out_shape = (
        jax.ShapeDtypeStruct((rows, cols), BF16),
        jax.ShapeDtypeStruct((RANK, rows // nrep), F32),
        jax.ShapeDtypeStruct((RANK, cols), BF16),
    )
    unit = half // 7
    widths = (2 * unit, 2 * unit, 3 * unit) * 2
    results = pl.pallas_call(
        functools.partial(kernel, geo),
        out_shape=tuple(jax.ShapeDtypeStruct((rows, wide), BF16) for wide in widths) + out_shape[1:],
        in_specs=[hbm_spec] * 3,
        out_specs=(any_spec,) * 8,
        scratch_shapes=[
            vmem((rows, cols), BF16), vmem((rows, cols), BF16), vmem((RANK, cols), BF16), vmem((rows, cols), BF16),
            vmem((2, nc, rows, core_rows), BF16), vmem((nc, nrep, piece, 2 * rows), BF16), vmem((rows, cols), BF16), vmem((RANK, cols), BF16), vmem((128, half), BF16),
            vmem((ITERS, ny, part, 128), F32), vmem((ITERS, ny, part, 128), F32),
            vmem((ITERS, part, 128), F32), vmem((ITERS, ny, part, 128), F32),
            vmem((ITERS, 2, part, 128), F32), vmem((ITERS, ny, part, 128), F32),
            vmem((ITERS, nc, TILE, 128), F32), vmem((ITERS, nb, TILE, 128), F32),
            vmem((ITERS, nc, TILE, 128), F32), vmem((RANK, 128), F32), vmem((6 * 128, 128), BF16),
            vmem((ITERS, nrep, piece, 128), F32), vmem((ITERS, nrep, piece, 128), F32),
            vmem((ITERS, owners, TILE, 128), F32), vmem((ITERS, chips, TILE, 128), F32),
            vmem((ITERS, nc, owners, TILE, 128), BF16), vmem((chips, TILE, 128), BF16),
            vmem((nrep, RANK, rows // nrep), F32), vmem((RANK, rows // nrep), F32),
            dma((9,)), dma((8,)), dma((stages, ITERS)), dma((stages, ITERS)), dma((ITERS, nrep)), dma((ITERS, nrep)),
        ],
        compiler_params=pltpu.CompilerParams(
            collective_id=0, has_side_effects=True, vmem_limit_bytes=(52 * 1024 + 640) * 1024
        ),
        name="power_step",
    )(gradients, errors, warm_factor)
    return pl.pallas_call(
        place,
        out_shape=out_shape,
        in_specs=[any_spec] * 8,
        out_specs=(any_spec,) * 3,
        scratch_shapes=[dma((8,))],
        compiler_params=pltpu.CompilerParams(vmem_limit_bytes=8 * 1024 * 1024),
        name="place",
    )(*results)


def build(mesh, geo):
    in_specs = (P("dp", "tensor"), P("dp", "tensor"), P(None, "tensor"))
    out_specs = (P("dp", "tensor"), P(None, "dp"), P(None, "tensor"))
    return jax.shard_map(
        functools.partial(step, geo), mesh=mesh, in_specs=in_specs, out_specs=out_specs, check_vma=False
    )


def solution(mesh):
    return build(mesh, (4, 2, 4, 2, 8))
```

```python
import functools

import jax
import jax.numpy as jnp
from jax import lax
from jax.experimental import pallas as pl
from jax.experimental.pallas import tpu as pltpu
from jax.sharding import PartitionSpec as P

ITERS = 2
MESH = pl.DeviceIdType.MESH
HIGH = lax.Precision.HIGHEST
F32 = jnp.float32
BF16 = jnp.bfloat16
RANK = 64
TILE = 16


def lanes(shape):
    return lax.broadcasted_iota(jnp.int32, shape, 1)


def spread(x):
    low = lanes(x.shape) < RANK
    turned = pltpu.roll(x, RANK, 1)
    zero = jnp.zeros_like(x)
    first = jnp.concatenate([jnp.where(low, x, zero), jnp.where(low, turned, zero)], axis=0)
    second = jnp.concatenate([jnp.where(low, zero, turned), jnp.where(low, zero, x)], axis=0)
    return first, second


def split2(x):
    hi = x.astype(BF16)
    return hi, (x - hi.astype(F32)).astype(BF16)


def split3(x):
    hi, rest = split2(x)
    mid = rest
    return hi, mid, (x - hi.astype(F32) - mid.astype(F32)).astype(BF16)


def six_left(x):
    hi, mid, lo = split3(x)
    return jnp.concatenate([hi, hi, mid, hi, lo, mid], axis=1)


def six_right(x):
    hi, mid, lo = split3(x)
    return jnp.concatenate([hi, mid, hi, lo, hi, mid], axis=0)


def eliminate(rows, out_ref):
    block = 16
    for k0 in range(0, RANK, block):
        n = rows.shape[0]
        cols = [jnp.broadcast_to(rows[:, k0 + j : k0 + j + 1], (n, 128)) for j in range(block)]
        for i in range(block):
            scale = lax.rsqrt(cols[i][i : i + 1, :])
            row = rows[i : i + 1, :] * scale
            out_ref[k0 + i : k0 + i + 1, :] = row
            if k0 + i == RANK - 1:
                break
            factor = cols[i] * scale
            rows = rows - factor * row
            for j in range(i + 1, block):
                cols[j] = cols[j] - factor * (cols[j][i : i + 1, :] * scale)
        rows = rows[block:, :] if n > block else rows


def kernel(
    geo, g_hbm, e_hbm, w_hbm, ne0, ne1, ne2, ne3, ne4, ne5, left_out, right_out,
    gv, ev, wv, cv, cs, ctv, nev, rv, qt,
    p_send, p_rs, p_own, p_far, p_near, p_n, p_tie, p_some, g_send, g_x, g_ag, chol, solver,
    q_send, q_core, q_sum, q_x, q_ag, size_ref, l_send, l_recv,
    load_sem, store_sem, send_sem, recv_sem, piece_send, piece_recv,
):
    ne_outs = (ne0, ne1, ne2, ne3, ne4, ne5)
    nrep, nzl, nx, nc, ny = geo
    nb = nzl * nx * nc
    nz = nrep * nzl
    chips = nz * nx
    owners = q_ag.shape[2]
    share = owners // nrep
    dp, y = lax.axis_index("dp"), lax.axis_index("tensor")
    c = lax.rem(dp, nc)
    b = lax.rem(dp, nb)
    rep = lax.div(dp, nb)
    chip = lax.div(dp, nc)
    x = lax.rem(chip, nx)
    z = lax.div(chip, nx)
    at_rep = lax.div(b, nc)
    owns = at_rep < share
    mine_at = rep * share + at_rep
    rows, cols = gv.shape
    half_rows, half = rows // 2, cols // 2
    partner = (dp + 1 - 2 * c, y)
    l_dst = nrep * b + rep
    moved = l_dst != dp

    def y_peers(act):
        for k in sorted(range(1, ny), key=lambda k: -min(k, ny - k)):
            j = lax.rem(y + k, ny)
            act(j, (dp, j))

    def far_peers(act):
        far = lax.rem(rep + nrep // 2, nrep) * nb + b
        for k in sorted(range(ny), key=lambda k: -min(k, ny - k)):
            j = lax.rem(y + k, ny)
            act(j, (far, j))

    def near_device(step):
        return (lax.rem(rep + nrep + step, nrep) * nb + b, y)

    def block_peers(act):
        for k in range(1, nb):
            j = lax.rem(b + k, nb)
            act(j, (rep * nb + j, y))

    def chip_peers(act):
        def at_z(i, carry):
            step = lax.div(i + 1, 2)
            to_z = lax.rem(z + nz // 2 + jnp.where(lax.rem(i, 2) == 1, nz - step, step), nz)
            for k in sorted(range(nx), key=lambda k: -min(k, nx - k)):
                j = to_z * nx + lax.rem(x + k, nx)
                if k == 0:
                    pl.when(j != chip)(functools.partial(act, j, (j * nc + c, y)))
                else:
                    act(j, (j * nc + c, y))
            return carry

        lax.fori_loop(0, nz, at_z, 0)

    barrier = pltpu.get_barrier_semaphore()

    def greet(device):
        pl.semaphore_signal(barrier, inc=1, device_id=device, device_id_type=MESH)

    y_peers(lambda j, device: greet(device))
    for k in range(1, nrep):
        greet((lax.rem(rep + k, nrep) * nb + b, y))
    block_peers(lambda j, device: greet(device))
    greeted = ny - 1 + nrep - 1 + nb - 1
    parts = [pl.ds(h * (rows // 4), rows // 4) for h in range(4)]
    pairs = [(w_hbm, wv)] + [(src.at[part], dst.at[part]) for part in parts for src, dst in ((g_hbm, gv), (e_hbm, ev))]
    loads = [pltpu.make_async_copy(src, dst, load_sem.at[i]) for i, (src, dst) in enumerate(pairs)]
    for load in loads:
        load.start()

    def remote(src, dst, stage, it, device):
        return pltpu.make_async_remote_copy(
            src_ref=src, dst_ref=dst, send_sem=send_sem.at[stage, it], recv_sem=recv_sem.at[stage, it],
            device_id=device, device_id_type=MESH,
        )

    pending = []

    def swap(stage, it, peers, src, slots, me, count):
        peers(lambda j, device: remote(src(j), slots.at[me], stage, it, device).start())
        whole = remote(slots.at[:count], slots.at[:count], stage, it, partner)
        pending.append(whole.wait_send)
        return whole.wait_recv

    def total(slots, n):
        return functools.reduce(jnp.add, [slots[j] for j in range(n)])

    loads[0].wait()
    q_packed = jnp.concatenate([wv[:, :half], wv[:, half:]], axis=0).T
    low = lanes((half_rows, 128)) < RANK

    for it in range(ITERS):
        if it == 0:
            ones, twos = [], []
            for h, part in enumerate(parts):
                loads[1 + 2 * h].wait()
                loads[2 + 2 * h].wait()
                cv[part] = (gv[part].astype(F32) + ev[part].astype(F32)).astype(BF16)
                ones.append(jnp.dot(cv[part, :half], q_packed, preferred_element_type=F32))
                twos.append(jnp.dot(cv[part, half:], q_packed, preferred_element_type=F32))
            one, two = jnp.concatenate(ones, axis=0), jnp.concatenate(twos, axis=0)
            packed = jnp.where(
                low,
                one[:half_rows] + pltpu.roll(two[:half_rows], RANK, 1),
                pltpu.roll(one[half_rows:], RANK, 1) + two[half_rows:],
            )
            one, two = jnp.concatenate(ones, axis=0), jnp.concatenate(twos, axis=0)
        else:
            own_q = q_ag[it - 1, c].reshape(half // nc, 128)
            one = jnp.dot(cs[0, c], own_q, preferred_element_type=F32)
            two = jnp.dot(cs[1, c], own_q, preferred_element_type=F32)
            wait_other()
            other_q = q_ag[it - 1, 1 - c].reshape(half // nc, 128)
            one += jnp.dot(cs[0, 1 - c], other_q, preferred_element_type=F32)
            two += jnp.dot(cs[1, 1 - c], other_q, preferred_element_type=F32)
        packed = jnp.where(
            low,
            one[:half_rows] + pltpu.roll(two[:half_rows], RANK, 1),
            pltpu.roll(one[half_rows:], RANK, 1) + two[half_rows:],
        )
        p_send[it] = packed.reshape(ny, half_rows // ny, 128)
        if it == 0:
            pl.semaphore_wait(barrier, greeted)
        tie_y = lax.rem(y + ny // 2, ny)
        mine = p_own.at[it]
        both = remote(p_near.at[it], p_near.at[it], 1, it, partner)
        if it == 0:
            wait = swap(0, it, y_peers, lambda j: p_send.at[it, j], p_rs.at[it], y, ny - 1)
            p_rs[it, y] = p_send[it, y]
            turned_c = cv[...].T.reshape(2, nc, nrep, -1, rows)
            for core in range(nc):
                for group in range(nrep):
                    ctv[core, group] = jnp.concatenate([turned_c[0, core, group], turned_c[1, core, group]], axis=1)
            for i in range(2 * nc):
                cs[i // nc, i % nc] = cv[:, i * (half // nc) : (i + 1) * (half // nc)]
            wait()
            mine[...] = total(p_rs.at[it], ny)
            for slot, step in ((1, 1), (0, -1)):
                remote(mine, p_near.at[it, slot], 1, it, near_device(step)).start()
        else:
            own_tie = remote(p_send.at[it, tie_y], p_tie.at[0], 3, it, (dp, tie_y))
            own_tie.start()
            for k in sorted(range(1, ny), key=lambda k: -min(k, ny - k)):
                if k != ny // 2:
                    j = lax.rem(y + k, ny)
                    remote(p_send.at[it, j], p_rs.at[it, y], 0, it, (dp, j)).start()
            for slot, step in ((2, 1), (1, -1)):
                to = lax.rem(rep + nrep + step, nrep) * nb + b
                remote(p_send.at[it, tie_y], p_tie.at[slot], 12, it, (to, tie_y)).start()
            rest = remote(p_rs.at[it, : ny - 2], p_rs.at[it, : ny - 2], 0, it, partner)
            near_ties = remote(p_tie.at[1:3], p_tie.at[1:3], 12, it, partner)
            pending.extend([rest.wait_send, own_tie.wait_send, near_ties.wait_send])
            rest.wait_recv()
            some = p_send[it, y]
            for k in range(1, ny):
                if k != ny // 2:
                    some = some + p_rs[it, lax.rem(y + k, ny)]
            p_some[...] = some
            for slot, step in ((1, 1), (0, -1)):
                remote(p_some, p_near.at[it, slot], 1, it, near_device(step)).start()
            own_tie.wait_recv()
            mine[...] = some + p_tie[0]
        pending.append(both.wait_send)
        wait_far = swap(2, it, far_peers, lambda j: mine, p_far.at[it], y, ny)
        both.wait_recv()
        near = p_near[it, 0] + p_near[it, 1]
        if it > 0:
            near_ties.wait_recv()
            near = near + (p_tie[1] + p_tie[2])
        p_n[it, y] = p_own[it] + near
        wait_near = swap(9, it, y_peers, lambda j: p_n.at[it, y], p_n.at[it], y, ny - 1)
        wait_far()
        wait_near()
        p_whole = (p_far[it] + p_n[it]).reshape(half_rows, 128)

        first, second = spread(p_whole)
        parts_of_p = jnp.concatenate(split2(jnp.concatenate([first, second], axis=0)), axis=1)

        def right_term(core, group):
            both = jnp.dot(ctv[core, group], parts_of_p, preferred_element_type=F32)
            return both[:, :128] + both[:, 128:]

        groups = [lax.rem(rep + k, nrep) for k in sorted(range(nrep), key=lambda k: -min(k, nrep - k))]
        pieces = []
        for i, group in enumerate(groups):
            q_send[it, i] = right_term(1 - c, group)
            pieces.append(
                pltpu.make_async_remote_copy(
                    src_ref=q_send.at[it, i], dst_ref=q_core.at[it, i], send_sem=piece_send.at[it, i],
                    recv_sem=piece_recv.at[it, i], device_id=partner, device_id_type=MESH,
                )
            )
            pieces[-1].start()
            pending.append(pieces[-1].wait_send)

        gram2 = lax.dot_general(
            p_whole, p_whole, (((0,), (0,)), ((), ())), precision=HIGH, preferred_element_type=F32
        )
        gram = gram2[:RANK] + pltpu.roll(gram2[RANK:], RANK, 1)
        low_t = lanes((TILE, 128)) < RANK
        for h in range(nc):
            upper, lower = gram[2 * h * TILE : (2 * h + 1) * TILE], gram[(2 * h + 1) * TILE : (2 * h + 2) * TILE]
            g_send[it, h] = jnp.where(low_t, upper, pltpu.roll(lower, RANK, 1))
        g_x[it, b] = g_send[it, c]
        wait_gram = swap(4, it, block_peers, lambda j: g_send.at[it, lax.rem(j, nc)], g_x.at[it], b, nb - 1)

        for i, group in enumerate(groups):
            own = right_term(c, group)
            pieces[i].wait_recv()
            q_sum[it, pl.ds(group * share, share)] = (own + q_core[it, i]).reshape(share, TILE, 128)
            for k in range(share):
                j = group * (nb // nc) + k

                @pl.when(j != chip)
                def _(j=j, k=k, group=group):
                    remote(q_sum.at[it, group * share + k], q_x.at[it, chip], 5, it, (j * nc + c, y)).start()

        wait_gram()
        g_ag[it, c] = total(g_x.at[it], nb)
        own_gram, other_gram = g_ag.at[it, c], g_ag.at[it, 1 - c]
        gram_copy = remote(own_gram, own_gram, 6, it, partner)
        gram_copy.start()
        pending.append(gram_copy.wait_send)
        remote(other_gram, other_gram, 6, it, partner).wait_recv()
        blocks = []
        for h in range(nc):
            whole = g_ag[it, h]
            blocks += [whole, pltpu.roll(whole, RANK, 1)]
        lane = lanes((RANK, 128))
        unit = (lane - RANK == lax.broadcasted_iota(jnp.int32, (RANK, 128), 0)).astype(F32)
        eliminate(jnp.where(lane < RANK, jnp.concatenate(blocks, axis=0), unit), chol)
        inverse = chol[...]
        turned = pltpu.roll(inverse, RANK, 1)
        solve = jnp.concatenate([jnp.where(lane < RANK, turned, 0.0), jnp.where(lane < RANK, 0.0, inverse)], axis=0)
        solver[...] = six_right(solve.T)

        def solved(x):
            return jnp.dot(six_left(x), solver[...], preferred_element_type=F32)

        @pl.when(owns)
        def _():
            q_x[it, chip] = q_sum[it, mine_at]
            most = q_x.at[it, : chips - 1]
            remote(most, most, 5, it, partner).wait_recv()
            mine = q_ag.at[it, c, mine_at]
            mine[...] = (solved(jnp.sum(q_x[it], axis=0)) / nrep).astype(BF16)
            for group in groups:
                stage = 11 if group is groups[0] else 7
                for k in range(nb // nc):
                    j = group * (nb // nc) + k

                    def send(j=j, stage=stage):
                        remote(mine, mine, stage, it, (j * nc + c, y)).start()

                    if group is groups[-1]:
                        pl.when(j != chip)(send)
                    else:
                        send()

        if it == ITERS - 1:
            left = solved(p_whole)
            turned_left = left.T
            per_half = nrep // 2
            wide = rows // nrep
            for r in range(nrep):
                h, o = r // per_half, r % per_half * wide
                l_send[r] = turned_left[h * RANK : (h + 1) * RANK, o : o + wide]
            l_copy = remote(l_send.at[rep], l_recv, 10, 0, (l_dst, y))

            @pl.when(moved)
            def _():
                l_copy.start()

            @pl.when(jnp.logical_not(moved))
            def _():
                l_recv[...] = l_send[rep]

            p_first, p_second = spread(left)
            p_first, p_second = p_first.astype(BF16), p_second.astype(BF16)

        most = size_ref.at[: (nrep - 1) * share]

        @pl.when(owns)
        def _():
            others = size_ref.at[: (nrep - 1) * share - 1]
            remote(others, others, 7, it, partner).wait_recv()

        @pl.when(jnp.logical_not(owns))
        def _():
            remote(most, most, 7, it, partner).wait_recv()

        for group in groups[1:] + groups[:1]:
            slab = q_ag.at[it, c, pl.ds(group * share, share)]
            passed = remote(slab, slab, 8, it, partner)
            if group is groups[0]:
                remote(slab, slab, 11, it, partner).wait_recv()
            passed.start()
        passed = remote(q_ag.at[it, c], q_ag.at[it, c], 8, it, partner)
        pending.append(passed.wait_send)
        wait_other = passed.wait_recv

    early = half // nc // 128 * 128
    late = half - early
    halves = ((0, p_first), (half, p_second))

    def renew(at, wide, q_part):
        for start, left_half in halves:
            span = pl.ds(pl.multiple_of(start + at, 128), wide)
            rebuilt = jnp.dot(left_half, q_part, preferred_element_type=F32)
            nev[:, span] = (gv[:, span].astype(F32) + ev[:, span].astype(F32) - rebuilt).astype(BF16)
            yield

    ahead = q_ag[ITERS - 1, c, pl.ds(c * ((late - half // nc) // TILE), early // TILE)]
    for _ in renew(c * late, early, ahead.reshape(early, 128).T):
        pass
    wait_other()
    q_turned = q_ag[ITERS - 1].reshape(half, 128).T
    qt[...] = q_turned
    rv[:, :half] = q_turned[:RANK]
    rv[:, half:] = q_turned[RANK:]
    stores = [pltpu.make_async_copy(rv, right_out, store_sem.at[0])]
    stores[0].start()
    per_half = len(ne_outs) // 2
    at = 0
    late_at = pl.multiple_of((1 - c) * early, 128)
    for h, _ in enumerate(renew(late_at, late, qt[:, pl.ds(late_at, late)])):
        for ne_out in ne_outs[h * per_half : (h + 1) * per_half]:
            wide = ne_out.shape[1]
            stores.append(pltpu.make_async_copy(nev.at[:, pl.ds(at, wide)], ne_out, store_sem.at[len(stores)]))
            stores[-1].start()
            at += wide

    @pl.when(moved)
    def _():
        l_copy.wait()

    stores.append(pltpu.make_async_copy(l_recv, left_out, store_sem.at[len(stores)]))
    stores[-1].start()
    sized = size_ref.at[: (nrep - 1) * (nb // nc) - 1]
    far_sized = size_ref.at[: nb // nc]
    for it in range(ITERS):

        @pl.when(owns)
        def _():
            most = q_sum.at[it, : owners - 1]
            remote(most, most, 5, it, partner).wait_send()
            remote(sized, sized, 7, it, partner).wait_send()
            remote(far_sized, far_sized, 11, it, partner).wait_send()

        @pl.when(jnp.logical_not(owns))
        def _():
            remote(q_sum.at[it], q_sum.at[it], 5, it, partner).wait_send()

    for done in pending:
        done()
    for store in stores:
        store.wait()


def place(*refs):
    *sources, new_errors, left, right, sem = refs
    pieces, targets, at = sources[:-2], [], 0
    for piece in pieces:
        targets.append(new_errors.at[:, pl.ds(at, piece.shape[1])])
        at += piece.shape[1]
    targets += [left, right]
    copies = [pltpu.make_async_copy(src, dst, sem.at[i]) for i, (src, dst) in enumerate(zip(sources, targets))]
    for copy in copies:
        copy.start()
    for copy in copies:
        copy.wait()


def step(geo, gradients, errors, warm_factor):
    nrep, nzl, nx, nc, ny = geo
    nb = nzl * nx * nc
    chips = nrep * nzl * nx
    rows, cols = gradients.shape
    half = cols // 2
    part = rows // 2 // ny
    core_rows = half // nc
    piece = core_rows // nrep
    owners = core_rows // TILE
    stages = 13
    dma = pltpu.SemaphoreType.DMA
    vmem = pltpu.VMEM
    any_spec = pl.BlockSpec(memory_space=pl.ANY)
    hbm_spec = pl.BlockSpec(memory_space=pltpu.HBM)
    out_shape = (
        jax.ShapeDtypeStruct((rows, cols), BF16),
        jax.ShapeDtypeStruct((RANK, rows // nrep), F32),
        jax.ShapeDtypeStruct((RANK, cols), BF16),
    )
    unit = half // 7
    widths = (2 * unit, 2 * unit, 3 * unit) * 2
    results = pl.pallas_call(
        functools.partial(kernel, geo),
        out_shape=tuple(jax.ShapeDtypeStruct((rows, wide), BF16) for wide in widths) + out_shape[1:],
        in_specs=[hbm_spec] * 3,
        out_specs=(any_spec,) * 8,
        scratch_shapes=[
            vmem((rows, cols), BF16), vmem((rows, cols), BF16), vmem((RANK, cols), BF16), vmem((rows, cols), BF16),
            vmem((2, nc, rows, core_rows), BF16), vmem((nc, nrep, piece, 2 * rows), BF16), vmem((rows, cols), BF16), vmem((RANK, cols), BF16), vmem((128, half), BF16),
            vmem((ITERS, ny, part, 128), F32), vmem((ITERS, ny, part, 128), F32),
            vmem((ITERS, part, 128), F32), vmem((ITERS, ny, part, 128), F32),
            vmem((ITERS, 2, part, 128), F32), vmem((ITERS, ny, part, 128), F32),
            vmem((3, part, 128), F32), vmem((part, 128), F32),
            vmem((ITERS, nc, TILE, 128), F32), vmem((ITERS, nb, TILE, 128), F32),
            vmem((ITERS, nc, TILE, 128), F32), vmem((RANK, 128), F32), vmem((6 * 128, 128), BF16),
            vmem((ITERS, nrep, piece, 128), F32), vmem((ITERS, nrep, piece, 128), F32),
            vmem((ITERS, owners, TILE, 128), F32), vmem((ITERS, chips, TILE, 128), F32),
            vmem((ITERS, nc, owners, TILE, 128), BF16), vmem((chips, TILE, 128), BF16),
            vmem((nrep, RANK, rows // nrep), F32), vmem((RANK, rows // nrep), F32),
            dma((9,)), dma((8,)), dma((stages, ITERS)), dma((stages, ITERS)), dma((ITERS, nrep)), dma((ITERS, nrep)),
        ],
        compiler_params=pltpu.CompilerParams(
            collective_id=0, has_side_effects=True, vmem_limit_bytes=(52 * 1024 + 640) * 1024
        ),
        name="power_step",
    )(gradients, errors, warm_factor)
    return pl.pallas_call(
        place,
        out_shape=out_shape,
        in_specs=[any_spec] * 8,
        out_specs=(any_spec,) * 3,
        scratch_shapes=[dma((8,))],
        compiler_params=pltpu.CompilerParams(vmem_limit_bytes=8 * 1024 * 1024),
        name="place",
    )(*results)


def build(mesh, geo):
    in_specs = (P("dp", "tensor"), P("dp", "tensor"), P(None, "tensor"))
    out_specs = (P("dp", "tensor"), P(None, "dp"), P(None, "tensor"))
    return jax.shard_map(
        functools.partial(step, geo), mesh=mesh, in_specs=in_specs, out_specs=out_specs, check_vma=False
    )


def solution(mesh):
    return build(mesh, (4, 2, 4, 2, 8))
```
